512 devices in a mesh: outer: 32 (over z, y_hi), inner: 16 (over x, y_lo, core).
Axes of the slice: x: 4, y: 8 (y_hi: 4, y_lo: 2; y = y_hi * 2 + y_lo), z: 8, core: 2. Of those that a mesh axis runs over, the one named last changes fastest.
Arguments:
- queries: bfloat16 [131072, 256], P(('outer', 'inner')), may hold values from -24 to 24, as said below
- keys: bfloat16 [131072, 256], P(('outer', 'inner')), may hold values from -24 to 24, as said below
- values: bfloat16 [131072, 256], P(('outer', 'inner')), may hold values from -6 to 6
- grad_out: bfloat16 [131072, 256], P(('outer', 'inner')), may hold values from -6 to 6
- group_lengths: int32 [256], replicated, may hold values from 1 to 1024, 131072 in all
Outputs:
- grad_queries: bfloat16 [131072, 256], P(('outer', 'inner'))
- grad_keys: bfloat16 [131072, 256], P(('outer', 'inner'))
- grad_values: bfloat16 [131072, 256], P(('outer', 'inner'))
The draws below stay inside these ranges and needn't reach their ends.
Inputs may be any that keep to these rules, and one draw needn't show every extreme that they name: `queries`: shown draw: independent entries; scores of order one. `keys`: shown draw: independent entries.
All inputs are finite; a program needn't handle non-finite values.
Results may differ from the reference program's by a relative error of at most 0.017.
Values may be sent and summed in bfloat16 or wider, within the bound.
No kernel may reach another device: no remote copies, remote signals or barrier semaphores. Data moves between devices by JAX's collectives and lax.ppermute only.
A program may use at most 64 MiB of HBM per device.

```python
import math
import jax
import jax.numpy as jnp
import numpy as np
from jax import lax

HEADS = 2
HD = 128
CTX = 2
TOK_DEV = 256
TOKENS = 131072
MOST = 1024
GROUPS = 256
REACH = 12


def draw_queries(key, part):
    key = jax.random.fold_in(key, 1)
    noise = jnp.clip(jax.random.normal(key, (TOKENS, HEADS * HD), jnp.float32), -6.0, 6.0)
    result = noise
    return result.astype(jnp.bfloat16)


def draw_keys(key, part):
    key = jax.random.fold_in(key, 2)
    noise = jnp.clip(jax.random.normal(key, (TOKENS, HEADS * HD), jnp.float32), -6.0, 6.0)
    result = noise
    return result.astype(jnp.bfloat16)


def shard_levels(rng, shape, pieces, smallest, top_value):
    def one(axis_at, blocks):
        steps = jax.random.uniform(jax.random.fold_in(jax.random.fold_in(rng, 6), axis_at), (blocks,), jnp.float32, smallest / len(pieces), top_value / len(pieces))
        return jnp.repeat(jnp.exp(steps), shape[axis_at] // blocks).reshape((-1,) + (1,) * (len(shape) - axis_at - 1))

    loudness = one(*pieces[0])
    for cut in pieces[1:]:
        loudness = loudness * one(*cut)
    return loudness


def split_up(number_of, total, most, slope):
    portions = [(1 << 20) // math.isqrt(standing ** slope) + 1 for standing in range(2, number_of + 1)]
    surplus, given = total - most - (number_of - 1), [1] * (number_of - 1)
    while surplus > 0:
        free = [i for i in range(number_of - 1) if given[i] < most]
        mass, remaining = sum([portions[i] for i in free]), surplus
        for i in free:
            extra = min(most - given[i], max(1, remaining * portions[i] // mass), surplus)
            given[i] = given[i] + extra
            surplus = surplus - extra
    return np.array([most] + given)


def uneven_parts(own_key, number_of, total, most, skew):
    if number_of == 2:
        one = jax.random.randint(own_key, (), max(1, total - most), min(most, total - 1) + 1)
        return jnp.stack([one, total - one])
    sizes = jnp.asarray(split_up(number_of, total, most, skew), jnp.int32)
    pairs = (number_of - 1) // 2
    giver, taker = sizes[1:1 + 2 * pairs:2], sizes[2:2 + 2 * pairs:2]
    margin = jnp.minimum(giver - 1, most - taker)
    moved = jax.random.randint(jax.random.fold_in(own_key, 1), (pairs,), 0, 1 << 20) % (margin + 1)
    sizes = sizes.at[1:1 + 2 * pairs:2].set(giver - moved).at[2:2 + 2 * pairs:2].set(taker + moved)
    return sizes[jax.random.permutation(jax.random.fold_in(own_key, 2), number_of)]


def bell_draw(rng, shape, scale, reach, split=(), held_as=jnp.bfloat16):
    drawn = scale * jax.random.normal(rng, shape, jnp.float32)
    if split:
        drawn = drawn * shard_levels(rng, shape, split, -0.22, 0.18)
    return jnp.clip(drawn, -reach, reach).astype(held_as)


def setup_inputs(seed: int = 0) -> dict:
    arg_keys = jax.random.split(jax.random.key(seed), 6)
    queries = draw_queries(jax.random.fold_in(arg_keys[5], 71), 0)
    keys = draw_keys(jax.random.fold_in(arg_keys[5], 71), 0)
    values = bell_draw(arg_keys[2], (TOKENS, HEADS * HD), 1.0, 6.0, ((0, 512),))
    grad_out = bell_draw(arg_keys[3], (TOKENS, HEADS * HD), 1.0, 6.0, ((0, 512),))
    group_lengths = uneven_parts(arg_keys[4], GROUPS, TOKENS, MOST, 1).astype(jnp.int32)
    return dict(queries=queries, keys=keys, values=values, grad_out=grad_out, group_lengths=group_lengths)


def group_of(pos, ends):
    return lax.optimization_barrier(jnp.sum((ends[None, :] <= pos[:, None]).astype(jnp.int32), axis=1))

def allowed_pairs(qpos, kpos, ends):
    cq = group_of(qpos, ends)
    ck = group_of(kpos, ends)
    valid = (kpos >= 0)[None, :]
    return valid & (ck[None, :] <= cq[:, None]) & (ck[None, :] >= cq[:, None] - CTX)

def reference(queries, keys, values, grad_out, group_lengths):
    rows = TOK_DEV
    pad = REACH * rows
    span = pad + rows
    width = HEADS * HD
    scale = 1.0 / math.sqrt(HD)
    ends = jnp.cumsum(group_lengths).astype(jnp.int32)
    keys_pad = jnp.pad(keys, ((pad, 0), (0, 0)))
    values_pad = jnp.pad(values, ((pad, 0), (0, 0)))

    def step(carry, block):
        dk_all, dv_all = carry
        start = (block * rows).astype(jnp.int32)
        qblk = lax.dynamic_slice_in_dim(queries, start, rows, 0).reshape(rows, HEADS, HD).astype(jnp.float32)
        gblk = lax.dynamic_slice_in_dim(grad_out, start, rows, 0).reshape(rows, HEADS, HD).astype(jnp.float32)
        kblk = lax.dynamic_slice_in_dim(keys_pad, start, span, 0).reshape(span, HEADS, HD).astype(jnp.float32)
        vblk = lax.dynamic_slice_in_dim(values_pad, start, span, 0).reshape(span, HEADS, HD).astype(jnp.float32)
        qpos = start + jnp.arange(rows, dtype=jnp.int32)
        kpos = start - pad + jnp.arange(span, dtype=jnp.int32)
        mask = allowed_pairs(qpos, kpos, ends)[None]
        scores = jnp.einsum('qhd,khd->hqk', qblk, kblk) * scale
        top = lax.optimization_barrier(jnp.max(jnp.where(mask, scores, -jnp.inf), axis=2))
        total = lax.optimization_barrier(jnp.sum(jnp.where(mask, jnp.exp(scores - top[:, :, None]), 0.0), axis=2))
        lse = top + jnp.log(total)
        probs = jnp.where(mask, jnp.exp(scores - lse[:, :, None]), 0.0)
        probs_b = probs.astype(jnp.bfloat16).astype(jnp.float32)
        output = jnp.einsum('hqk,khd->qhd', probs_b, vblk)
        delta = jnp.einsum('qhd,qhd->hq', gblk, output)
        dprobs = jnp.einsum('qhd,khd->hqk', gblk, vblk)
        dscores = (probs * (dprobs - delta[:, :, None])).astype(jnp.bfloat16).astype(jnp.float32)
        dv_term = jnp.einsum('hqk,qhd->khd', probs_b, gblk).reshape(span, width)
        dk_term = (jnp.einsum('hqk,qhd->khd', dscores, qblk) * scale).reshape(span, width)
        dq_term = (jnp.einsum('hqk,khd->qhd', dscores, kblk) * scale).reshape(rows, width)
        dk_all = lax.dynamic_update_slice_in_dim(dk_all, lax.dynamic_slice_in_dim(dk_all, start, span, 0) + dk_term, start, 0)
        dv_all = lax.dynamic_update_slice_in_dim(dv_all, lax.dynamic_slice_in_dim(dv_all, start, span, 0) + dv_term, start, 0)
        return ((dk_all, dv_all), dq_term.astype(jnp.bfloat16))
    zeros = jnp.zeros((TOKENS + pad, width), jnp.float32)
    blocks = jnp.arange(TOKENS // rows, dtype=jnp.int32)
    (dk_all, dv_all), dq_blocks = lax.scan(step, (zeros, zeros), blocks)
    grad_queries = dq_blocks.reshape(TOKENS, width)
    return (grad_queries, dk_all[pad:].astype(jnp.bfloat16), dv_all[pad:].astype(jnp.bfloat16))
```

```python
import functools
import math

import jax
import jax.numpy as jnp
from jax import lax
from jax.experimental import pallas as pl
from jax.experimental.pallas import tpu as pltpu
from jax.sharding import PartitionSpec as P

HEADS = 2
HD = 128
CTX = 2
BLK = 256
NX, NY, NC = 4, 2, 2
ROW = NX * NY * NC
COL = NY * NC
NQ = NX * NC
NEG = -1e30
LOG2E = math.log2(math.e)

XC_GROUPS = [[x * 4 + y * 2 + c for x in range(NX) for c in range(NC)] for y in range(NY)]
COL_GROUPS = [[x * 4 + y * 2 + c for y in range(NY) for c in range(NC)] for x in range(NX)]
X_GROUPS = [[x * 4 + k for x in range(NX)] for k in range(COL)]


def exchange(value, groups):
    return lax.all_to_all(value, "inner", 0, 0, axis_index_groups=groups, tiled=True)


def row_step(value, steps):
    count = lax.axis_size("outer")
    first, last = max(0, -steps), min(count, count - steps)
    return lax.ppermute(value, "outer", [(i, i + steps) for i in range(first, last)])


def by_head(left, right):
    return jnp.stack(
        [
            jnp.concatenate([left[:, h * HD : (h + 1) * HD], right[:, h * HD : (h + 1) * HD]], axis=1)
            for h in range(HEADS)
        ]
    )


def key_ranges(group_lengths, row, y_lo):
    ends = jnp.cumsum(group_lengths).astype(jnp.int32)
    x = jnp.arange(NX, dtype=jnp.int32)[:, None, None]
    c = jnp.arange(NC, dtype=jnp.int32)[None, :, None]
    i = jnp.arange(BLK, dtype=jnp.int32)[None, None, :]
    first = (row * ROW + x * COL + y_lo * NC + c) * BLK
    pos = (first + i).reshape(NQ, BLK)
    last = (first + BLK + 0 * i).reshape(NQ, BLK)
    e = ends[:, None, None]
    low = jnp.max(jnp.where(e[CTX:] <= pos[None], e[:-CTX], 0), axis=0)
    high = jnp.min(jnp.where(e > pos[None], e, jnp.int32(1 << 30)), axis=0)
    return low, jnp.minimum(high, last)


def tile_terms(kv_ref, qg_ref, lohi_ref, n, t, base):
    rows = pl.ds(pl.multiple_of(t * BLK, BLK), BLK)
    k = kv_ref[rows, :HD]
    v = kv_ref[rows, HD:]
    q = qg_ref[n, :, :HD]
    g = qg_ref[n, :, HD:]
    dims = (((1,), (1,)), ((), ()))
    s = lax.dot_general(k, q, dims, preferred_element_type=jnp.float32) * (LOG2E / math.sqrt(HD))
    dp = lax.dot_general(v, g, dims, preferred_element_type=jnp.float32)
    pos = base + t * BLK + lax.broadcasted_iota(jnp.int32, (BLK, BLK), 0)
    lohi = lohi_ref[n]
    allowed = (pos >= lohi[0:1]) & (pos < lohi[1:2])
    return jnp.where(allowed, s, NEG), dp, q, g, rows


def stats_kernel(info_ref, qg_ref, kva_ref, kvb_ref, lohi_ref, out_ref):
    x = info_ref[0]

    def run(kv_ref, base, first, last):
        def block(n, _):
            def tile(t, carry):
                m, l, u = carry
                s, dp, _, _, _ = tile_terms(kv_ref, qg_ref, lohi_ref, n, t, base)
                m_new = jnp.maximum(m, jnp.max(s, axis=0, keepdims=True))
                keep = jnp.exp2(m - m_new)
                e = jnp.exp2(s - m_new)
                l = l * keep + jnp.sum(e, axis=0, keepdims=True)
                u = u * keep + jnp.sum(e * dp, axis=0, keepdims=True)
                return m_new, l, u

            zero = jnp.zeros((1, BLK), jnp.float32)
            m, l, u = lax.fori_loop(
                info_ref[8 + n], info_ref[16 + n], tile, (jnp.full((1, BLK), NEG, jnp.float32), zero, zero)
            )
            l = jnp.where(m > 0.5 * NEG, l, 1.0)
            out_ref[n, 0:1] = m + jnp.log2(l)
            out_ref[n, 1:2] = u / l
            return 0

        lax.fori_loop(first, last, block, 0)

    run(kvb_ref, info_ref[2], 0, x * NC)
    run(kva_ref, info_ref[1], x * NC, NQ)


def grads_kernel(
    info_ref, qg_ref, kva_ref, kvb_ref, lohi_ref, stats_ref, dq_ref, da_ref, db_ref, ka_ref, kb_ref, acca_ref, accb_ref
):
    x = info_ref[0]
    scale = 1.0 / math.sqrt(HD)
    ka_ref[...] = kva_ref[:, :HD].T
    kb_ref[...] = kvb_ref[:, :HD].T
    acca_ref[...] = jnp.zeros_like(acca_ref)
    accb_ref[...] = jnp.zeros_like(accb_ref)

    def run(kv_ref, kt_ref, acc_ref, base, first, last):
        def block(n, _):
            part = [stats_ref[i, n] for i in range(NX)]
            top = functools.reduce(jnp.maximum, [p[0:1] for p in part])
            weights = [jnp.exp2(p[0:1] - top) for p in part]
            total = sum(weights)
            lse = top + jnp.log2(total)
            delta = sum(w * p[1:2] for w, p in zip(weights, part)) / total

            def tile(t, dq):
                s, dp, q, g, rows = tile_terms(kv_ref, qg_ref, lohi_ref, n, t, base)
                p = jnp.exp2(s - lse)
                pb = p.astype(jnp.bfloat16)
                ds = (p * (dp - delta)).astype(jnp.bfloat16)
                dims = (((1,), (0,)), ((), ()))
                acc_ref[rows, HD:] += lax.dot_general(pb, g, dims, preferred_element_type=jnp.float32)
                acc_ref[rows, :HD] += lax.dot_general(ds, q, dims, preferred_element_type=jnp.float32)
                return dq + lax.dot_general(kt_ref[:, rows], ds, dims, preferred_element_type=jnp.float32)

            dq = lax.fori_loop(info_ref[8 + n], info_ref[16 + n], tile, jnp.zeros((HD, BLK), jnp.float32))
            dq_ref[n] = (dq * scale).astype(jnp.bfloat16)
            return 0

        lax.fori_loop(first, last, block, 0)

    run(kvb_ref, kb_ref, accb_ref, info_ref[2], 0, x * NC)
    run(kva_ref, ka_ref, acca_ref, info_ref[1], x * NC, NQ)
    for i in range(COL):
        rows = slice(i * BLK, (i + 1) * BLK)
        for out_ref, acc_ref in ((da_ref, acca_ref), (db_ref, accb_ref)):
            out_ref[i, :, :HD] = (acc_ref[rows, :HD] * scale).astype(jnp.bfloat16)
            out_ref[i, :, HD:] = acc_ref[rows, HD:].astype(jnp.bfloat16)


SMEM = pl.BlockSpec(memory_space=pltpu.SMEM)
VMEM = pl.BlockSpec(memory_space=pltpu.VMEM)


def per_device(queries, keys, values, grad_out, group_lengths):
    row = lax.axis_index("outer").astype(jnp.int32)
    inner = lax.axis_index("inner").astype(jnp.int32)
    x, y_lo = inner // COL, inner // NC % NY

    kv = by_head(keys, values)
    kv_before = row_step(kv, 1)
    qg = jnp.broadcast_to(by_head(queries, grad_out)[None], (NX, HEADS, BLK, 2 * HD))
    qg = exchange(qg.reshape(NQ, BLK, 2 * HD), XC_GROUPS)

    def column(value):
        return exchange(jnp.broadcast_to(value[None], (NY,) + value.shape).reshape(COL, BLK, 2 * HD), COL_GROUPS)

    kva = column(kv).reshape(COL * BLK, 2 * HD)
    kvb = column(kv_before).reshape(COL * BLK, 2 * HD)

    low, high = key_ranges(group_lengths, row, y_lo)
    lohi = jnp.stack([low, high], axis=1)
    base_a = (row * ROW + x * COL) * BLK
    base_b = base_a - ROW * BLK
    base = jnp.where(jnp.arange(NQ, dtype=jnp.int32) < x * NC, base_b, base_a)
    tile_first = jnp.clip((low[:, 0] - base) // BLK, 0, COL)
    tile_last = jnp.clip((high[:, -1] - base + BLK - 1) // BLK, 0, COL)
    info = jnp.concatenate([jnp.stack([x, base_a, base_b, row, x, x, x, x]), tile_first, tile_last]).astype(jnp.int32)

    params = pltpu.CompilerParams(vmem_limit_bytes=48 * 1024 * 1024)
    stats = pl.pallas_call(
        stats_kernel,
        out_shape=jax.ShapeDtypeStruct((NQ, 2, BLK), jnp.float32),
        in_specs=[SMEM, VMEM, VMEM, VMEM, VMEM],
        out_specs=VMEM,
        compiler_params=params,
        cost_estimate=pl.CostEstimate(flops=16 * 2 * 2 * BLK * BLK * HD, bytes_accessed=2 << 20, transcendentals=16 * BLK * BLK),
        name="stats",
    )(info, qg, kva, kvb, lohi)

    stats = exchange(jnp.broadcast_to(stats[None], (NX,) + stats.shape), X_GROUPS)

    dq, da, db = pl.pallas_call(
        grads_kernel,
        out_shape=(
            jax.ShapeDtypeStruct((NQ, HD, BLK), jnp.bfloat16),
            jax.ShapeDtypeStruct((COL, BLK, 2 * HD), jnp.bfloat16),
            jax.ShapeDtypeStruct((COL, BLK, 2 * HD), jnp.bfloat16),
        ),
        in_specs=[SMEM, VMEM, VMEM, VMEM, VMEM, VMEM],
        out_specs=(VMEM, VMEM, VMEM),
        scratch_shapes=[
            pltpu.VMEM((HD, COL * BLK), jnp.bfloat16),
            pltpu.VMEM((HD, COL * BLK), jnp.bfloat16),
            pltpu.VMEM((COL * BLK, 2 * HD), jnp.float32),
            pltpu.VMEM((COL * BLK, 2 * HD), jnp.float32),
        ],
        compiler_params=params,
        cost_estimate=pl.CostEstimate(flops=16 * 5 * 2 * BLK * BLK * HD, bytes_accessed=4 << 20, transcendentals=16 * BLK * BLK),
        name="grads",
    )(info, qg, kva, kvb, lohi, stats)

    def owners(value):
        value = exchange(value, COL_GROUPS).reshape(NY, HEADS, BLK, 2 * HD)
        return jnp.sum(value.astype(jnp.float32), axis=0)

    from_next = row_step(owners(db).astype(jnp.bfloat16), -1)
    dq = exchange(dq, XC_GROUPS).reshape(NX, HEADS, HD, BLK)
    dq = jnp.sum(dq.astype(jnp.float32), axis=0).astype(jnp.bfloat16)
    grad_q = jnp.transpose(dq, (2, 0, 1)).reshape(BLK, HEADS * HD)
    dkv = (owners(da) + from_next.astype(jnp.float32)).astype(jnp.bfloat16)
    grad_k = jnp.concatenate([dkv[h, :, :HD] for h in range(HEADS)], axis=1)
    grad_v = jnp.concatenate([dkv[h, :, HD:] for h in range(HEADS)], axis=1)
    return grad_q, grad_k, grad_v


def solution(mesh):
    placed = P(("outer", "inner"), None)
    return jax.shard_map(
        per_device,
        mesh=mesh,
        in_specs=(placed, placed, placed, placed, P()),
        out_specs=(placed, placed, placed),
        check_vma=False,
    )
```

```python
import functools
import math

import jax
import jax.numpy as jnp
from jax import lax
from jax.experimental import pallas as pl
from jax.experimental.pallas import tpu as pltpu
from jax.sharding import PartitionSpec as P

HEADS = 2
HD = 128
CTX = 2
BLK = 256
NX, NY, NC = 4, 2, 2
ROW = NX * NY * NC
COL = NY * NC
NQ = NX * NC
NEG = -1e30
UNROLL = 4
LOG2E = math.log2(math.e)

XC_GROUPS = [[x * 4 + y * 2 + c for x in range(NX) for c in range(NC)] for y in range(NY)]
X_GROUPS = [[x * 4 + k for x in range(NX)] for k in range(COL)]


def exchange(value, groups):
    return lax.all_to_all(value, "inner", 0, 0, axis_index_groups=groups, tiled=True)


def row_step(value, steps):
    count = lax.axis_size("outer")
    first, last = max(0, -steps), min(count, count - steps)
    return lax.ppermute(value, "outer", [(i, i + steps) for i in range(first, last)])


def partner(value, flip):
    return lax.ppermute(value, "inner", [(i ^ flip, i) for i in range(ROW)])


def key_ranges(group_lengths, row, y_lo, core):
    ends = jnp.cumsum(group_lengths).astype(jnp.int32)
    x = jnp.arange(NX, dtype=jnp.int32)[:, None, None]
    c = jnp.arange(NC, dtype=jnp.int32)[None, :, None] ^ core
    i = jnp.arange(BLK, dtype=jnp.int32)[None, None, :]
    first = (row * ROW + x * COL + y_lo * NC + c) * BLK
    pos = (first + i).reshape(NQ, BLK)
    last = (first + BLK + 0 * i).reshape(NQ, BLK)
    e = ends[:, None, None]
    low = jnp.max(jnp.where(e[CTX:] <= pos[None], e[:-CTX], 0), axis=0)
    high = jnp.min(jnp.where(e > pos[None], e, jnp.int32(1 << 30)), axis=0)
    return low, jnp.minimum(high, last)


def list_tiles(info_ref, tiles_ref):
    x = info_ref[0]
    count = jnp.int32(0)
    for n in range(NQ):
        before = n // NC < x
        row = jnp.where(before, COL * BLK, 0)
        pos = jnp.where(before, info_ref[2], info_ref[1])

        def put(t, i, n=n, row=row, pos=pos):
            tiles_ref[0, i] = n
            tiles_ref[1, i] = row + t * BLK
            tiles_ref[2, i] = pos + t * BLK
            return i + 1

        count = lax.fori_loop(info_ref[8 + n], info_ref[16 + n], put, count)
    for i in range(UNROLL - 1):
        tiles_ref[0, count + i] = 0
        tiles_ref[1, count + i] = 0
        tiles_ref[2, count + i] = -(1 << 30)
    return (count + UNROLL - 1) // UNROLL


def tile_terms(tiles_ref, i, kv_ref, qg_ref, lohi_ref):
    n, row, pos = tiles_ref[0, i], tiles_ref[1, i], tiles_ref[2, i]
    rows = pl.ds(pl.multiple_of(row, BLK), BLK)
    k = kv_ref[rows, :HD]
    v = kv_ref[rows, HD:]
    q = qg_ref[n, :, :HD]
    g = qg_ref[n, :, HD:]
    dims = (((1,), (1,)), ((), ()))
    s = lax.dot_general(k, q, dims, preferred_element_type=jnp.float32) * (LOG2E / math.sqrt(HD))
    dp = lax.dot_general(v, g, dims, preferred_element_type=jnp.float32)
    key = lax.broadcasted_iota(jnp.int32, (BLK, BLK), 0)
    low, high = lohi_ref[n, 0:1] - pos, lohi_ref[n, 1:2] - pos
    return n, rows, q, g, jnp.where((key >= low) & (key < high), s, NEG), dp


def pack_kernel(info_ref, q_ref, k_ref, v_ref, g_ref, give_ref, kv_ref, qg_ref):
    core = info_ref[0]
    refs = (k_ref, v_ref, q_ref, g_ref)
    for c in range(NC):

        @pl.when(core == c)
        def _():
            for i, ref in enumerate(refs):
                give_ref[:, i * HD : (i + 1) * HD] = ref[:, (1 - c) * HD : (2 - c) * HD]
                mine_ref = (kv_ref, qg_ref)[i // 2]
                mine_ref[:, i % 2 * HD : (i % 2 + 1) * HD] = ref[:, c * HD : (c + 1) * HD]


def assemble(y_lo, core, own_ref, other_ref, out_ref, start):
    for y, ref in ((y_lo, own_ref), (1 - y_lo, other_ref)):
        for i in range(NC):
            row = start + (y * NC + (core ^ i)) * BLK
            out_ref[pl.ds(pl.multiple_of(row, BLK), BLK)] = ref[i]


def stats_kernel(
    info_ref, qg_ref, kva_own_ref, kva_other_ref, kvb_own_ref, kvb_other_ref, lohi_ref,
    out_ref, tiles_ref, kv_ref, m_ref, l_ref, u_ref,
):
    y_lo, core = info_ref[3], info_ref[4]
    pairs = list_tiles(info_ref, tiles_ref)
    assemble(y_lo, core, kva_own_ref, kva_other_ref, kv_ref, 0)
    assemble(y_lo, core, kvb_own_ref, kvb_other_ref, kv_ref, COL * BLK)
    m_ref[...] = jnp.full_like(m_ref, NEG)
    l_ref[...] = jnp.zeros_like(l_ref)
    u_ref[...] = jnp.zeros_like(u_ref)

    def step(i, _):
        terms = [tile_terms(tiles_ref, UNROLL * i + j, kv_ref, qg_ref, lohi_ref) for j in range(UNROLL)]
        parts = []
        for n, _, _, _, s, dp in terms:
            m = jnp.max(s, axis=0, keepdims=True)
            e = jnp.exp2(s - m)
            parts.append((n, m, jnp.sum(e, axis=0, keepdims=True), jnp.sum(e * dp, axis=0, keepdims=True)))
        for n, m, l, u in parts:
            old = m_ref[n]
            new = jnp.maximum(old, m)
            keep, add = jnp.exp2(old - new), jnp.exp2(m - new)
            m_ref[n] = new
            l_ref[n] = l_ref[n] * keep + l * add
            u_ref[n] = u_ref[n] * keep + u * add
        return 0

    lax.fori_loop(0, pairs, step, 0)
    for n in range(NQ):
        m = m_ref[n]
        l = jnp.where(m > 0.5 * NEG, l_ref[n], 1.0)
        lse, delta = m + jnp.log2(l), u_ref[n] / l
        for i in range(NX):
            out_ref[i, n, 0:1] = lse
            out_ref[i, n, 1:2] = delta


def grads_kernel(
    info_ref, qg_ref, kva_own_ref, kva_other_ref, kvb_own_ref, kvb_other_ref, lohi_ref, stats_ref,
    dq_ref, own_a_ref, own_b_ref, away_a_ref, away_b_ref,
    tiles_ref, kv_ref, kt_ref, acc_ref, dqt_ref, sums_ref,
):
    y_lo, core = info_ref[3], info_ref[4]
    scale = 1.0 / math.sqrt(HD)
    pairs = list_tiles(info_ref, tiles_ref)
    assemble(y_lo, core, kva_own_ref, kva_other_ref, kv_ref, 0)
    assemble(y_lo, core, kvb_own_ref, kvb_other_ref, kv_ref, COL * BLK)
    kt_ref[...] = kv_ref[:, :HD].T
    acc_ref[...] = jnp.zeros_like(acc_ref)
    dqt_ref[...] = jnp.zeros_like(dqt_ref)
    for n in range(NQ):
        part = [stats_ref[i, n] for i in range(NX)]
        top = functools.reduce(jnp.maximum, [p[0:1] for p in part])
        weights = [jnp.exp2(p[0:1] - top) for p in part]
        total = sum(weights)
        sums_ref[n, 0:1] = top + jnp.log2(total)
        sums_ref[n, 1:2] = sum(w * p[1:2] for w, p in zip(weights, part)) / total

    def step(i, _):
        terms = [tile_terms(tiles_ref, UNROLL * i + j, kv_ref, qg_ref, lohi_ref) for j in range(UNROLL)]
        parts = []
        for n, rows, q, g, s, dp in terms:
            p = jnp.exp2(s - sums_ref[n, 0:1])
            pb = p.astype(jnp.bfloat16)
            ds = (p * (dp - sums_ref[n, 1:2])).astype(jnp.bfloat16)
            dims = (((1,), (0,)), ((), ()))
            dv = lax.dot_general(pb, g, dims, preferred_element_type=jnp.float32)
            dk = lax.dot_general(ds, q, dims, preferred_element_type=jnp.float32)
            dq = lax.dot_general(kt_ref[:, rows], ds, dims, preferred_element_type=jnp.float32)
            parts.append((n, rows, dk, dv, dq))
        for n, rows, dk, dv, dq in parts:
            acc_ref[rows, :HD] += dk
            acc_ref[rows, HD:] += dv
            dqt_ref[n] += dq
        return 0

    lax.fori_loop(0, pairs, step, 0)
    for n in range(NQ):
        dq_ref[n ^ core] = (dqt_ref[n] * scale).astype(jnp.bfloat16)
    for i in range(NC):
        for start, own_ref, away_ref in ((0, own_a_ref, away_a_ref), (COL * BLK, own_b_ref, away_b_ref)):
            for y, out_ref in ((y_lo, own_ref), (1 - y_lo, away_ref)):
                rows = pl.ds(pl.multiple_of(start + (y * NC + (core ^ i)) * BLK, BLK), BLK)
                out_ref[i, :, :HD] = (acc_ref[rows, :HD] * scale).astype(out_ref.dtype)
                out_ref[i, :, HD:] = acc_ref[rows, HD:].astype(out_ref.dtype)


def finish_kernel(
    info_ref, own_a_ref, got_a_ref, mate_a_ref, next_ref, dq_ref, grad_q_ref, grad_k_ref, grad_v_ref
):
    core = info_ref[0]
    f32 = jnp.float32
    mine = own_a_ref[0] + got_a_ref[0].astype(f32) + next_ref[0].astype(f32)
    other = mate_a_ref[...].astype(f32) + next_ref[1].astype(f32)
    for c in range(NC):

        @pl.when(core == c)
        def _():
            for h, part in ((c, mine), (1 - c, other)):
                cols = slice(h * HD, (h + 1) * HD)
                grad_k_ref[:, cols] = part[:, :HD].astype(jnp.bfloat16)
                grad_v_ref[:, cols] = part[:, HD:].astype(jnp.bfloat16)

    for h in range(HEADS):
        dq = sum(dq_ref[i * HEADS + h].astype(f32) for i in range(NX))
        grad_q_ref[:, h * HD : (h + 1) * HD] = dq.T.astype(jnp.bfloat16)


SMEM = pl.BlockSpec(memory_space=pltpu.SMEM)
VMEM = pl.BlockSpec(memory_space=pltpu.VMEM)
PARAMS = pltpu.CompilerParams(vmem_limit_bytes=24 * 1024 * 1024)


def stats_call(info, qg, kv, lohi):
    return pl.pallas_call(
        stats_kernel,
        out_shape=jax.ShapeDtypeStruct((NX, NQ, 2, BLK), jnp.float32),
        in_specs=[SMEM] + [VMEM] * 6,
        out_specs=VMEM,
        scratch_shapes=[
            pltpu.SMEM((3, NQ * COL + UNROLL), jnp.int32),
            pltpu.VMEM((2 * COL * BLK, 2 * HD), jnp.bfloat16),
        ]
        + [pltpu.VMEM((NQ, 1, BLK), jnp.float32)] * 3,
        compiler_params=PARAMS,
        cost_estimate=pl.CostEstimate(flops=16 * 2 * 2 * BLK * BLK * HD, bytes_accessed=2 << 20, transcendentals=16 * BLK * BLK),
        name="stats",
    )(info, qg, *kv, lohi)


def grads_call(info, qg, kv, lohi, stats):
    part = (NC, BLK, 2 * HD)
    return pl.pallas_call(
        grads_kernel,
        out_shape=(
            jax.ShapeDtypeStruct((NQ, HD, BLK), jnp.bfloat16),
            jax.ShapeDtypeStruct(part, jnp.float32),
            jax.ShapeDtypeStruct(part, jnp.float32),
            jax.ShapeDtypeStruct(part, jnp.bfloat16),
            jax.ShapeDtypeStruct(part, jnp.bfloat16),
        ),
        in_specs=[SMEM] + [VMEM] * 7,
        out_specs=(VMEM,) * 5,
        scratch_shapes=[
            pltpu.SMEM((3, NQ * COL + UNROLL), jnp.int32),
            pltpu.VMEM((2 * COL * BLK, 2 * HD), jnp.bfloat16),
            pltpu.VMEM((HD, 2 * COL * BLK), jnp.bfloat16),
            pltpu.VMEM((2 * COL * BLK, 2 * HD), jnp.float32),
            pltpu.VMEM((NQ, HD, BLK), jnp.float32),
            pltpu.VMEM((NQ, 2, BLK), jnp.float32),
        ],
        compiler_params=PARAMS,
        cost_estimate=pl.CostEstimate(flops=16 * 5 * 2 * BLK * BLK * HD, bytes_accessed=4 << 20, transcendentals=16 * BLK * BLK),
        name="grads",
    )(info, qg, *kv, lohi, stats)


def per_device(queries, keys, values, grad_out, group_lengths):
    row = lax.axis_index("outer").astype(jnp.int32)
    inner = lax.axis_index("inner").astype(jnp.int32)
    x, y_lo, core = inner // COL, inner // NC % NY, inner % NC

    bf16 = jnp.bfloat16
    me = core[None]
    give, kv_mine, qg_mine = pl.pallas_call(
        pack_kernel,
        out_shape=(
            jax.ShapeDtypeStruct((BLK, 4 * HD), bf16),
            jax.ShapeDtypeStruct((BLK, 2 * HD), bf16),
            jax.ShapeDtypeStruct((BLK, 2 * HD), bf16),
        ),
        in_specs=[SMEM] + [VMEM] * 4,
        out_specs=(VMEM,) * 3,
        compiler_params=pltpu.CompilerParams(vmem_limit_bytes=60 * 1024 * 1024),
        cost_estimate=pl.CostEstimate(flops=0, bytes_accessed=1 << 20, transcendentals=0),
        name="pack",
    )(me, queries, keys, values, grad_out)
    got = partner(give, 1)

    kva = jnp.stack([kv_mine, got[:, : 2 * HD]])
    kvb = row_step(kva, 1)
    kva, got = lax.optimization_barrier((kva, got))
    qg = jnp.broadcast_to(jnp.stack([qg_mine, got[:, 2 * HD :]])[None], (NX, NC, BLK, 2 * HD))
    qg, group_lengths = lax.optimization_barrier((qg, group_lengths))
    qg = exchange(qg, X_GROUPS).reshape(NQ, BLK, 2 * HD)
    kv = [kva, partner(kva, 2), kvb, partner(kvb, 2)]

    low, high = key_ranges(group_lengths, row, y_lo, core)
    lohi = jnp.stack([low, high], axis=1)
    base_a = (row * ROW + x * COL) * BLK
    base_b = base_a - ROW * BLK
    base = jnp.where(jnp.arange(NQ, dtype=jnp.int32) < x * NC, base_b, base_a)
    tile_first = jnp.clip((low[:, 0] - base) // BLK, 0, COL)
    tile_last = jnp.clip((high[:, -1] - base + BLK - 1) // BLK, 0, COL)
    info = jnp.concatenate([jnp.stack([x, base_a, base_b, y_lo, core, x, x, x]), tile_first, tile_last]).astype(jnp.int32)

    stats = stats_call(info, qg, kv, lohi)
    stats = exchange(stats, X_GROUPS)

    dq, own_a, own_b, away_a, away_b = grads_call(info, qg, kv, lohi, stats)

    got_b = partner(away_b, 2)
    dq = exchange(dq, XC_GROUPS)
    sum_b = (own_b + got_b.astype(jnp.float32)).astype(bf16)
    sum_b, away_a = lax.optimization_barrier((sum_b, away_a))
    got_a = partner(away_a, 2)
    mate_b, dq = lax.optimization_barrier((partner(sum_b[1], 1), dq))
    from_next = row_step(jnp.stack([sum_b[0], mate_b]), -1)
    mate_a = partner((own_a[1] + got_a[1].astype(jnp.float32)).astype(bf16), 1)
    return pl.pallas_call(
        finish_kernel,
        out_shape=(jax.ShapeDtypeStruct((BLK, HEADS * HD), bf16),) * 3,
        in_specs=[SMEM] + [VMEM] * 5,
        out_specs=(VMEM,) * 3,
        compiler_params=PARAMS,
        cost_estimate=pl.CostEstimate(flops=0, bytes_accessed=2 << 20, transcendentals=0),
        name="finish",
    )(me, own_a, got_a, mate_a, from_next, dq)


def solution(mesh):
    placed = P(("outer", "inner"), None)
    return jax.shard_map(
        per_device,
        mesh=mesh,
        in_specs=(placed, placed, placed, placed, P()),
        out_specs=(placed, placed, placed),
        check_vma=False,
    )
```

```python
import functools
import math

import jax
import jax.numpy as jnp
from jax import lax
from jax.experimental import pallas as pl
from jax.experimental.pallas import tpu as pltpu
from jax.sharding import PartitionSpec as P

HEADS = 2
HD = 128
CTX = 2
BLK = 256
NX, NY, NC = 4, 2, 2
ROW = NX * NY * NC
COL = NY * NC
NQ = NX * NC
NEG = -1e30
UNROLL = 4
LOG2E = math.log2(math.e)

XC_GROUPS = [[x * 4 + y * 2 + c for x in range(NX) for c in range(NC)] for y in range(NY)]
X_GROUPS = [[x * 4 + k for x in range(NX)] for k in range(COL)]


def exchange(value, groups):
    return lax.all_to_all(value, "inner", 0, 0, axis_index_groups=groups, tiled=True)


def row_step(value, steps, flip=0):
    count = lax.axis_size("outer")
    first, last = max(0, -steps), min(count, count - steps)
    route = [(r * ROW + i, (r + steps) * ROW + (i ^ flip)) for r in range(first, last) for i in range(ROW)]
    return lax.ppermute(value, ("outer", "inner"), route)


def partner(value, flip):
    return lax.ppermute(value, "inner", [(i ^ flip, i) for i in range(ROW)])


def key_ranges(group_lengths, row, y_lo):
    ends = jnp.cumsum(group_lengths).astype(jnp.int32)
    x = jnp.arange(NX, dtype=jnp.int32)[:, None, None]
    c = jnp.arange(NC, dtype=jnp.int32)[None, :, None]
    i = jnp.arange(BLK, dtype=jnp.int32)[None, None, :]
    first = (row * ROW + x * COL + y_lo * NC + c) * BLK
    pos = (first + i).reshape(NQ, BLK)
    last = (first + BLK + 0 * i).reshape(NQ, BLK)
    e = ends[:, None, None]
    low = jnp.max(jnp.where(e[CTX:] <= pos[None], e[:-CTX], 0), axis=0)
    high = jnp.min(jnp.where(e > pos[None], e, jnp.int32(1 << 30)), axis=0)
    return low, jnp.minimum(high, last)


def list_tiles(info_ref, tiles_ref):
    x = info_ref[0]
    count = jnp.int32(0)
    for n in range(NQ):
        before = n // NC < x
        row = jnp.where(before, COL * BLK, 0)
        pos = jnp.where(before, info_ref[2], info_ref[1])

        def put(t, i, n=n, row=row, pos=pos):
            tiles_ref[0, i] = n
            tiles_ref[1, i] = row + t * BLK
            tiles_ref[2, i] = pos + t * BLK
            return i + 1

        count = lax.fori_loop(info_ref[8 + n], info_ref[16 + n], put, count)
    for i in range(UNROLL - 1):
        tiles_ref[0, count + i] = 0
        tiles_ref[1, count + i] = 0
        tiles_ref[2, count + i] = -(1 << 30)
    return (count + UNROLL - 1) // UNROLL


def tile_terms(tiles_ref, i, kv_ref, qg_ref, lohi_ref):
    n, row, pos = tiles_ref[0, i], tiles_ref[1, i], tiles_ref[2, i]
    rows = pl.ds(pl.multiple_of(row, BLK), BLK)
    k = kv_ref[rows, :HD]
    v = kv_ref[rows, HD:]
    q = qg_ref[n, :, :HD]
    g = qg_ref[n, :, HD:]
    dims = (((1,), (1,)), ((), ()))
    s = lax.dot_general(k, q, dims, preferred_element_type=jnp.float32) * (LOG2E / math.sqrt(HD))
    dp = lax.dot_general(v, g, dims, preferred_element_type=jnp.float32)
    key = lax.broadcasted_iota(jnp.int32, (BLK, BLK), 0)
    low = lohi_ref[n, 0:1]
    width = (lohi_ref[n, 1:2] - low).astype(jnp.uint32)
    allowed = (key - (low - pos)).astype(jnp.uint32) < width
    return n, rows, q, g, jnp.where(allowed, s, NEG), dp


def split_kernel(info_ref, k_ref, v_ref, mine_ref, give_ref):
    core = info_ref[0]
    for c in range(NC):

        @pl.when(core == c)
        def _():
            for i, ref in enumerate((k_ref, v_ref)):
                cols = slice(i * HD, (i + 1) * HD)
                mine_ref[:, cols] = ref[:, c * HD : (c + 1) * HD]
                give_ref[:, cols] = ref[:, (1 - c) * HD : (2 - c) * HD]


def pack_kernel(q_ref, g_ref, qg_ref):
    for n in range(NQ):
        head = slice(n % HEADS * HD, (n % HEADS + 1) * HD)
        qg_ref[n, :, :HD] = q_ref[:, head]
        qg_ref[n, :, HD:] = g_ref[:, head]


def assemble(y_lo, core, refs, out_ref):
    for j, ref in enumerate(refs):
        y = y_lo ^ (j // NC % NY)
        row = j // COL * COL * BLK + (y * NC + (core ^ (j % NC))) * BLK
        out_ref[pl.ds(pl.multiple_of(row, BLK), BLK)] = ref[...]


def stats_kernel(
    info_ref, qg_ref, a0_ref, a1_ref, a23_ref, b0_ref, b1_ref, b2_ref, b3_ref, lohi_ref,
    out_ref, tiles_ref, kv_ref, m_ref, l_ref, u_ref,
):
    y_lo, core = info_ref[3], info_ref[4]
    pairs = list_tiles(info_ref, tiles_ref)
    blocks = (a0_ref, a1_ref, a23_ref.at[0], a23_ref.at[1], b0_ref, b1_ref, b2_ref, b3_ref)
    assemble(y_lo, core, blocks, kv_ref)
    m_ref[...] = jnp.full_like(m_ref, NEG)
    l_ref[...] = jnp.zeros_like(l_ref)
    u_ref[...] = jnp.zeros_like(u_ref)

    def step(i, _):
        terms = [tile_terms(tiles_ref, UNROLL * i + j, kv_ref, qg_ref, lohi_ref) for j in range(UNROLL)]
        parts = []
        for n, _, _, _, s, dp in terms:
            m = jnp.max(s, axis=0, keepdims=True)
            e = jnp.exp2(s - m)
            parts.append((n, m, jnp.sum(e, axis=0, keepdims=True), jnp.sum(e * dp, axis=0, keepdims=True)))
        for n, m, l, u in parts:
            old = m_ref[n]
            new = jnp.maximum(old, m)
            keep, add = jnp.exp2(old - new), jnp.exp2(m - new)
            m_ref[n] = new
            l_ref[n] = l_ref[n] * keep + l * add
            u_ref[n] = u_ref[n] * keep + u * add
        return 0

    lax.fori_loop(0, pairs, step, 0)
    for n in range(NQ):
        m = m_ref[n]
        l = jnp.where(m > 0.5 * NEG, l_ref[n], 1.0)
        lse, delta = m + jnp.log2(l), u_ref[n] / l
        for i in range(NX):
            out_ref[i, n, 0:1] = lse
            out_ref[i, n, 1:2] = delta


def grads_kernel(
    info_ref, qg_ref, a0_ref, a1_ref, a23_ref, b0_ref, b1_ref, b2_ref, b3_ref, lohi_ref, stats_ref,
    dq_ref, own_a_ref, own_b_ref, away_a_ref, away_b_ref,
    tiles_ref, kv_ref, kt_ref, acc_ref, dqt_ref, sums_ref,
):
    y_lo, core = info_ref[3], info_ref[4]
    scale = 1.0 / math.sqrt(HD)
    pairs = list_tiles(info_ref, tiles_ref)
    blocks = (a0_ref, a1_ref, a23_ref.at[0], a23_ref.at[1], b0_ref, b1_ref, b2_ref, b3_ref)
    assemble(y_lo, core, blocks, kv_ref)
    kt_ref[...] = kv_ref[:, :HD].T
    acc_ref[...] = jnp.zeros_like(acc_ref)
    dqt_ref[...] = jnp.zeros_like(dqt_ref)
    for n in range(NQ):
        part = [stats_ref[i, n] for i in range(NX)]
        top = functools.reduce(jnp.maximum, [p[0:1] for p in part])
        weights = [jnp.exp2(p[0:1] - top) for p in part]
        total = sum(weights)
        sums_ref[n, 0:1] = top + jnp.log2(total)
        sums_ref[n, 1:2] = sum(w * p[1:2] for w, p in zip(weights, part)) / total

    def step(i, _):
        terms = [tile_terms(tiles_ref, UNROLL * i + j, kv_ref, qg_ref, lohi_ref) for j in range(UNROLL)]
        parts = []
        for n, rows, q, g, s, dp in terms:
            p = jnp.exp2(s - sums_ref[n, 0:1])
            pb = p.astype(jnp.bfloat16)
            ds = (p * (dp - sums_ref[n, 1:2])).astype(jnp.bfloat16)
            dims = (((1,), (0,)), ((), ()))
            dv = lax.dot_general(pb, g, dims, preferred_element_type=jnp.float32)
            dk = lax.dot_general(ds, q, dims, preferred_element_type=jnp.float32)
            dq = lax.dot_general(kt_ref[:, rows], ds, dims, preferred_element_type=jnp.float32)
            parts.append((n, rows, dk, dv, dq))
        for n, rows, dk, dv, dq in parts:
            acc_ref[rows, :HD] += dk
            acc_ref[rows, HD:] += dv
            dqt_ref[n] += dq
        return 0

    lax.fori_loop(0, pairs, step, 0)
    for n in range(NQ):
        dq_ref[n] = (dqt_ref[n] * scale).astype(jnp.bfloat16)
    for i in range(NC):
        for start, own_ref, away_ref in ((0, own_a_ref, away_a_ref), (COL * BLK, own_b_ref, away_b_ref)):
            for y, out_ref in ((y_lo, own_ref), (1 - y_lo, away_ref)):
                rows = pl.ds(pl.multiple_of(start + (y * NC + (core ^ i)) * BLK, BLK), BLK)
                out_ref[i, :, :HD] = (acc_ref[rows, :HD] * scale).astype(out_ref.dtype)
                out_ref[i, :, HD:] = acc_ref[rows, HD:].astype(out_ref.dtype)


def finish_kernel(
    info_ref, own_a_ref, got_a_ref, mate_a_ref, next_mine_ref, next_other_ref, dq_ref, grad_q_ref, grad_k_ref, grad_v_ref
):
    core = info_ref[0]
    f32 = jnp.float32
    mine = own_a_ref[0] + got_a_ref[0].astype(f32) + next_mine_ref[...].astype(f32)
    other = mate_a_ref[...].astype(f32) + next_other_ref[...].astype(f32)
    for c in range(NC):

        @pl.when(core == c)
        def _():
            for h, part in ((c, mine), (1 - c, other)):
                cols = slice(h * HD, (h + 1) * HD)
                grad_k_ref[:, cols] = part[:, :HD].astype(jnp.bfloat16)
                grad_v_ref[:, cols] = part[:, HD:].astype(jnp.bfloat16)

    for h in range(HEADS):
        dq = sum(dq_ref[i * HEADS + h].astype(f32) for i in range(NX))
        grad_q_ref[:, h * HD : (h + 1) * HD] = dq.T.astype(jnp.bfloat16)


SMEM = pl.BlockSpec(memory_space=pltpu.SMEM)
VMEM = pl.BlockSpec(memory_space=pltpu.VMEM)
PARAMS = pltpu.CompilerParams(vmem_limit_bytes=24 * 1024 * 1024)


def stats_call(info, qg, kv, lohi):
    return pl.pallas_call(
        stats_kernel,
        out_shape=jax.ShapeDtypeStruct((NX, NQ, 2, BLK), jnp.float32),
        in_specs=[SMEM] + [VMEM] * 9,
        out_specs=VMEM,
        scratch_shapes=[
            pltpu.SMEM((3, NQ * COL + UNROLL), jnp.int32),
            pltpu.VMEM((2 * COL * BLK, 2 * HD), jnp.bfloat16),
        ]
        + [pltpu.VMEM((NQ, 1, BLK), jnp.float32)] * 3,
        compiler_params=PARAMS,
        cost_estimate=pl.CostEstimate(flops=16 * 2 * 2 * BLK * BLK * HD, bytes_accessed=2 << 20, transcendentals=16 * BLK * BLK),
        name="stats",
    )(info, qg, *kv, lohi)


def grads_call(info, qg, kv, lohi, stats):
    part = (NC, BLK, 2 * HD)
    return pl.pallas_call(
        grads_kernel,
        out_shape=(
            jax.ShapeDtypeStruct((NQ, HD, BLK), jnp.bfloat16),
            jax.ShapeDtypeStruct(part, jnp.float32),
            jax.ShapeDtypeStruct(part, jnp.float32),
            jax.ShapeDtypeStruct(part, jnp.bfloat16),
            jax.ShapeDtypeStruct(part, jnp.bfloat16),
        ),
        in_specs=[SMEM] + [VMEM] * 10,
        out_specs=(VMEM,) * 5,
        scratch_shapes=[
            pltpu.SMEM((3, NQ * COL + UNROLL), jnp.int32),
            pltpu.VMEM((2 * COL * BLK, 2 * HD), jnp.bfloat16),
            pltpu.VMEM((HD, 2 * COL * BLK), jnp.bfloat16),
            pltpu.VMEM((2 * COL * BLK, 2 * HD), jnp.float32),
            pltpu.VMEM((NQ, HD, BLK), jnp.float32),
            pltpu.VMEM((NQ, 2, BLK), jnp.float32),
        ],
        compiler_params=PARAMS,
        cost_estimate=pl.CostEstimate(flops=16 * 5 * 2 * BLK * BLK * HD, bytes_accessed=4 << 20, transcendentals=16 * BLK * BLK),
        name="grads",
    )(info, qg, *kv, lohi, stats)


def per_device(queries, keys, values, grad_out, group_lengths):
    row = lax.axis_index("outer").astype(jnp.int32)
    inner = lax.axis_index("inner").astype(jnp.int32)
    x, y_lo, core = inner // COL, inner // NC % NY, inner % NC

    bf16 = jnp.bfloat16
    me = core[None]
    big = pltpu.CompilerParams(vmem_limit_bytes=60 * 1024 * 1024)
    mine, give = pl.pallas_call(
        split_kernel,
        out_shape=(jax.ShapeDtypeStruct((BLK, 2 * HD), bf16),) * 2,
        in_specs=[SMEM] + [VMEM] * 2,
        out_specs=(VMEM,) * 2,
        compiler_params=big,
        cost_estimate=pl.CostEstimate(flops=0, bytes_accessed=1 << 19, transcendentals=0),
        name="split",
    )(me, keys, values)
    qg = pl.pallas_call(
        pack_kernel,
        out_shape=jax.ShapeDtypeStruct((NQ, BLK, 2 * HD), bf16),
        in_specs=[VMEM] * 2,
        out_specs=VMEM,
        compiler_params=big,
        cost_estimate=pl.CostEstimate(flops=0, bytes_accessed=1 << 20, transcendentals=0),
        name="pack",
    )(queries, grad_out)

    b0, b1 = row_step(mine, 1), row_step(give, 1, 1)
    a1 = partner(give, 1)
    qg = exchange(qg, XC_GROUPS)
    a23 = partner(jnp.stack([mine, a1]), 2)
    b3, group_lengths = lax.optimization_barrier((partner(b1, 2), group_lengths))
    kv = [mine, a1, a23, b0, b1, partner(b0, 2), b3]

    low, high = key_ranges(group_lengths, row, y_lo)
    lohi = jnp.stack([low, high], axis=1)
    base_a = (row * ROW + x * COL) * BLK
    base_b = base_a - ROW * BLK
    base = jnp.where(jnp.arange(NQ, dtype=jnp.int32) < x * NC, base_b, base_a)
    tile_first = jnp.clip((low[:, 0] - base) // BLK, 0, COL)
    tile_last = jnp.clip((high[:, -1] - base + BLK - 1) // BLK, 0, COL)
    info = jnp.concatenate([jnp.stack([x, base_a, base_b, y_lo, core, x, x, x]), tile_first, tile_last]).astype(jnp.int32)

    stats = stats_call(info, qg, kv, lohi)
    stats = exchange(stats, X_GROUPS)

    dq, own_a, own_b, away_a, away_b = grads_call(info, qg, kv, lohi, stats)

    got_b = partner(away_b, 2)
    dq = exchange(dq, XC_GROUPS)
    mine_b, other_b = [(own_b[i] + got_b[i].astype(jnp.float32)).astype(bf16) for i in range(NC)]
    mine_b, other_b, away_a = lax.optimization_barrier((mine_b, other_b, away_a))
    next_mine = row_step(mine_b, -1)
    other_b, dq = lax.optimization_barrier((other_b, dq))
    next_other = row_step(other_b, -1, 1)
    got_a = partner(away_a, 2)
    mate_a = partner((own_a[1] + got_a[1].astype(jnp.float32)).astype(bf16), 1)
    return pl.pallas_call(
        finish_kernel,
        out_shape=(jax.ShapeDtypeStruct((BLK, HEADS * HD), bf16),) * 3,
        in_specs=[SMEM] + [VMEM] * 6,
        out_specs=(VMEM,) * 3,
        compiler_params=PARAMS,
        cost_estimate=pl.CostEstimate(flops=0, bytes_accessed=2 << 20, transcendentals=0),
        name="finish",
    )(me, own_a, got_a, mate_a, next_mine, next_other, dq)


def solution(mesh):
    placed = P(("outer", "inner"), None)
    return jax.shard_map(
        per_device,
        mesh=mesh,
        in_specs=(placed, placed, placed, placed, P()),
        out_specs=(placed, placed, placed),
        check_vma=False,
    )
```

```python
import functools
import math

import jax
import jax.numpy as jnp
from jax import lax
from jax.experimental import pallas as pl
from jax.experimental.pallas import tpu as pltpu
from jax.sharding import PartitionSpec as P

HEADS = 2
HD = 128
CTX = 2
BLK = 256
NX, NY, NC = 4, 2, 2
ROW = NX * NY * NC
COL = NY * NC
NQ = NX * NC
NEG = -1e30
UNROLL = 4
LOG2E = math.log2(math.e)

XC_GROUPS = [[x * 4 + y * 2 + c for x in range(NX) for c in range(NC)] for y in range(NY)]
X_GROUPS = [[x * 4 + k for x in range(NX)] for k in range(COL)]


def exchange(value, groups):
    return lax.all_to_all(value, "inner", 0, 0, axis_index_groups=groups, tiled=True)


def row_step(value, steps, flip=0):
    count = lax.axis_size("outer")
    first, last = max(0, -steps), min(count, count - steps)
    route = [(r * ROW + i, (r + steps) * ROW + (i ^ flip)) for r in range(first, last) for i in range(ROW)]
    return lax.ppermute(value, ("outer", "inner"), route)


def partner(value, flip):
    return lax.ppermute(value, "inner", [(i ^ flip, i) for i in range(ROW)])


def key_ranges(group_lengths, row, y_lo):
    ends = jnp.cumsum(group_lengths).astype(jnp.int32)
    x = jnp.arange(NX, dtype=jnp.int32)[:, None, None]
    c = jnp.arange(NC, dtype=jnp.int32)[None, :, None]
    i = jnp.arange(BLK, dtype=jnp.int32)[None, None, :]
    first = (row * ROW + x * COL + y_lo * NC + c) * BLK
    pos = (first + i).reshape(NQ, BLK)
    last = (first + BLK + 0 * i).reshape(NQ, BLK)
    e = ends[:, None, None]
    low = jnp.max(jnp.where(e[CTX:] <= pos[None], e[:-CTX], 0), axis=0)
    high = jnp.min(jnp.where(e > pos[None], e, jnp.int32(1 << 30)), axis=0)
    return low, jnp.minimum(high, last)


def list_tiles(info_ref, tiles_ref):
    x = info_ref[0]
    count = jnp.int32(0)
    for n in range(NQ):
        before = n // NC < x
        row = jnp.where(before, COL * BLK, 0)
        pos = jnp.where(before, info_ref[2], info_ref[1])

        def put(t, i, n=n, row=row, pos=pos):
            tiles_ref[0, i] = n
            tiles_ref[1, i] = row + t * BLK
            tiles_ref[2, i] = pos + t * BLK
            return i + 1

        count = lax.fori_loop(info_ref[8 + n], info_ref[16 + n], put, count)
    for i in range(UNROLL - 1):
        tiles_ref[0, count + i] = 0
        tiles_ref[1, count + i] = 0
        tiles_ref[2, count + i] = -(1 << 30)
    return (count + UNROLL - 1) // UNROLL


def tile_terms(tiles_ref, i, kv_ref, qg_ref, lohi_ref):
    n, row, pos = tiles_ref[0, i], tiles_ref[1, i], tiles_ref[2, i]
    rows = pl.ds(pl.multiple_of(row, BLK), BLK)
    k = kv_ref[rows, :HD]
    v = kv_ref[rows, HD:]
    q = qg_ref[n, :, :HD]
    g = qg_ref[n, :, HD:]
    dims = (((1,), (1,)), ((), ()))
    s = lax.dot_general(k, q, dims, preferred_element_type=jnp.float32) * (LOG2E / math.sqrt(HD))
    dp = lax.dot_general(v, g, dims, preferred_element_type=jnp.float32)
    key = lax.broadcasted_iota(jnp.int32, (BLK, BLK), 0)
    low = lohi_ref[n, 0:1]
    width = (lohi_ref[n, 1:2] - low).astype(jnp.uint32)
    allowed = (key - (low - pos)).astype(jnp.uint32) < width
    return n, rows, q, g, jnp.where(allowed, s, NEG), dp


def split_kernel(info_ref, k_ref, v_ref, mine_ref, give_ref):
    core = info_ref[0]
    for c in range(NC):

        @pl.when(core == c)
        def _():
            for i, ref in enumerate((k_ref, v_ref)):
                cols = slice(i * HD, (i + 1) * HD)
                mine_ref[:, cols] = ref[:, c * HD : (c + 1) * HD]
                give_ref[:, cols] = ref[:, (1 - c) * HD : (2 - c) * HD]


def pack_kernel(q_ref, g_ref, qg_ref):
    for n in range(NQ):
        head = slice(n % HEADS * HD, (n % HEADS + 1) * HD)
        qg_ref[n, :, :HD] = q_ref[:, head]
        qg_ref[n, :, HD:] = g_ref[:, head]


def assemble(y_lo, core, refs, out_ref):
    for j, ref in enumerate(refs):
        y = y_lo ^ (j // NC % NY)
        row = j // COL * COL * BLK + (y * NC + (core ^ (j % NC))) * BLK
        out_ref[pl.ds(pl.multiple_of(row, BLK), BLK)] = ref[...]


def stats_kernel(
    info_ref, qg_ref, a0_ref, a1_ref, a23_ref, b0_ref, b1_ref, b2_ref, b3_ref, lohi_ref,
    out_ref, tiles_ref, kv_ref, m_ref, l_ref, u_ref,
):
    y_lo, core = info_ref[3], info_ref[4]
    pairs = list_tiles(info_ref, tiles_ref)
    blocks = (a0_ref, a1_ref, a23_ref.at[0], a23_ref.at[1], b0_ref, b1_ref, b2_ref, b3_ref)
    assemble(y_lo, core, blocks, kv_ref)
    m_ref[...] = jnp.full_like(m_ref, NEG)
    l_ref[...] = jnp.zeros_like(l_ref)
    u_ref[...] = jnp.zeros_like(u_ref)

    def step(i, _):
        terms = [tile_terms(tiles_ref, UNROLL * i + j, kv_ref, qg_ref, lohi_ref) for j in range(UNROLL)]
        parts = []
        for n, _, _, _, s, dp in terms:
            m = jnp.max(s, axis=0, keepdims=True)
            e = jnp.exp2(s - m)
            parts.append((n, m, jnp.sum(e, axis=0, keepdims=True), jnp.sum(e * dp, axis=0, keepdims=True)))
        for n, m, l, u in parts:
            old = m_ref[n]
            new = jnp.maximum(old, m)
            keep, add = jnp.exp2(old - new), jnp.exp2(m - new)
            m_ref[n] = new
            l_ref[n] = l_ref[n] * keep + l * add
            u_ref[n] = u_ref[n] * keep + u * add
        return 0

    lax.fori_loop(0, pairs, step, 0)
    for n in range(NQ):
        m = m_ref[n]
        l = jnp.where(m > 0.5 * NEG, l_ref[n], 1.0)
        lse, delta = m + jnp.log2(l), u_ref[n] / l
        for i in range(NX):
            out_ref[i, n, 0:1] = lse
            out_ref[i, n, 1:2] = delta


def grads_kernel(
    info_ref, qg_ref, a0_ref, a1_ref, a23_ref, b0_ref, b1_ref, b2_ref, b3_ref, lohi_ref, stats_ref,
    dq_ref, own_a_ref, own_b_ref, away_a_ref, away_b_ref,
    tiles_ref, kv_ref, kt_ref, acc_ref, dqt_ref, sums_ref,
):
    y_lo, core = info_ref[3], info_ref[4]
    scale = 1.0 / math.sqrt(HD)
    pairs = list_tiles(info_ref, tiles_ref)
    blocks = (a0_ref, a1_ref, a23_ref.at[0], a23_ref.at[1], b0_ref, b1_ref, b2_ref, b3_ref)
    assemble(y_lo, core, blocks, kv_ref)
    kt_ref[...] = kv_ref[:, :HD].T
    acc_ref[...] = jnp.zeros_like(acc_ref)
    dqt_ref[...] = jnp.zeros_like(dqt_ref)
    for n in range(NQ):
        part = [stats_ref[i, n] for i in range(NX)]
        top = functools.reduce(jnp.maximum, [p[0:1] for p in part])
        weights = [jnp.exp2(p[0:1] - top) for p in part]
        total = sum(weights)
        sums_ref[n, 0:1] = top + jnp.log2(total)
        sums_ref[n, 1:2] = sum(w * p[1:2] for w, p in zip(weights, part)) / total

    def step(i, _):
        terms = [tile_terms(tiles_ref, UNROLL * i + j, kv_ref, qg_ref, lohi_ref) for j in range(UNROLL)]
        parts = []
        for n, rows, q, g, s, dp in terms:
            p = jnp.exp2(s - sums_ref[n, 0:1])
            pb = p.astype(jnp.bfloat16)
            ds = (p * (dp - sums_ref[n, 1:2])).astype(jnp.bfloat16)
            dims = (((1,), (0,)), ((), ()))
            dv = lax.dot_general(pb, g, dims, preferred_element_type=jnp.float32)
            dk = lax.dot_general(ds, q, dims, preferred_element_type=jnp.float32)
            dq = lax.dot_general(kt_ref[:, rows], ds, dims, preferred_element_type=jnp.float32)
            parts.append((n, rows, dk, dv, dq))
        for n, rows, dk, dv, dq in parts:
            acc_ref[rows, :HD] += dk
            acc_ref[rows, HD:] += dv
            dqt_ref[n] += dq
        return 0

    lax.fori_loop(0, pairs, step, 0)
    for n in range(NQ):
        dq_ref[n] = (dqt_ref[n] * scale).astype(jnp.bfloat16)
    for i in range(NC):
        for start, own_ref, away_ref in ((0, own_a_ref, away_a_ref), (COL * BLK, own_b_ref, away_b_ref)):
            for y, out_ref in ((y_lo, own_ref), (1 - y_lo, away_ref)):
                rows = pl.ds(pl.multiple_of(start + (y * NC + (core ^ i)) * BLK, BLK), BLK)
                out_ref[i, :, :HD] = (acc_ref[rows, :HD] * scale).astype(out_ref.dtype)
                out_ref[i, :, HD:] = acc_ref[rows, HD:].astype(out_ref.dtype)


def finish_kernel(
    info_ref, own_a_ref, got_a_ref, mate_a_ref, next_mine_ref, next_other_ref, dq_ref, grad_q_ref, grad_k_ref, grad_v_ref
):
    core = info_ref[0]
    f32 = jnp.float32
    mine = own_a_ref[0] + got_a_ref[0].astype(f32) + next_mine_ref[...].astype(f32)
    other = mate_a_ref[...].astype(f32) + next_other_ref[...].astype(f32)
    for c in range(NC):

        @pl.when(core == c)
        def _():
            for h, part in ((c, mine), (1 - c, other)):
                cols = slice(h * HD, (h + 1) * HD)
                grad_k_ref[:, cols] = part[:, :HD].astype(jnp.bfloat16)
                grad_v_ref[:, cols] = part[:, HD:].astype(jnp.bfloat16)

    for h in range(HEADS):
        dq = sum(dq_ref[i * HEADS + h].astype(f32) for i in range(NX))
        grad_q_ref[:, h * HD : (h + 1) * HD] = dq.T.astype(jnp.bfloat16)


SMEM = pl.BlockSpec(memory_space=pltpu.SMEM)
VMEM = pl.BlockSpec(memory_space=pltpu.VMEM)
PARAMS = pltpu.CompilerParams(vmem_limit_bytes=24 * 1024 * 1024)


def stats_call(info, qg, kv, lohi):
    return pl.pallas_call(
        stats_kernel,
        out_shape=jax.ShapeDtypeStruct((NX, NQ, 2, BLK), jnp.float32),
        in_specs=[SMEM] + [VMEM] * 9,
        out_specs=VMEM,
        scratch_shapes=[
            pltpu.SMEM((3, NQ * COL + UNROLL), jnp.int32),
            pltpu.VMEM((2 * COL * BLK, 2 * HD), jnp.bfloat16),
        ]
        + [pltpu.VMEM((NQ, 1, BLK), jnp.float32)] * 3,
        compiler_params=PARAMS,
        cost_estimate=pl.CostEstimate(flops=16 * 2 * 2 * BLK * BLK * HD, bytes_accessed=2 << 20, transcendentals=16 * BLK * BLK),
        name="stats",
    )(info, qg, *kv, lohi)


def grads_call(info, qg, kv, lohi, stats):
    part = (NC, BLK, 2 * HD)
    return pl.pallas_call(
        grads_kernel,
        out_shape=(
            jax.ShapeDtypeStruct((NQ, HD, BLK), jnp.bfloat16),
            jax.ShapeDtypeStruct(part, jnp.float32),
            jax.ShapeDtypeStruct(part, jnp.float32),
            jax.ShapeDtypeStruct(part, jnp.bfloat16),
            jax.ShapeDtypeStruct(part, jnp.bfloat16),
        ),
        in_specs=[SMEM] + [VMEM] * 10,
        out_specs=(VMEM,) * 5,
        scratch_shapes=[
            pltpu.SMEM((3, NQ * COL + UNROLL), jnp.int32),
            pltpu.VMEM((2 * COL * BLK, 2 * HD), jnp.bfloat16),
            pltpu.VMEM((HD, 2 * COL * BLK), jnp.bfloat16),
            pltpu.VMEM((2 * COL * BLK, 2 * HD), jnp.float32),
            pltpu.VMEM((NQ, HD, BLK), jnp.float32),
            pltpu.VMEM((NQ, 2, BLK), jnp.float32),
        ],
        compiler_params=PARAMS,
        cost_estimate=pl.CostEstimate(flops=16 * 5 * 2 * BLK * BLK * HD, bytes_accessed=4 << 20, transcendentals=16 * BLK * BLK),
        name="grads",
    )(info, qg, *kv, lohi, stats)


def per_device(queries, keys, values, grad_out, group_lengths):
    row = lax.axis_index("outer").astype(jnp.int32)
    inner = lax.axis_index("inner").astype(jnp.int32)
    x, y_lo, core = inner // COL, inner // NC % NY, inner % NC

    bf16 = jnp.bfloat16
    me = core[None]
    big = pltpu.CompilerParams(vmem_limit_bytes=60 * 1024 * 1024)
    mine, give = pl.pallas_call(
        split_kernel,
        out_shape=(jax.ShapeDtypeStruct((BLK, 2 * HD), bf16),) * 2,
        in_specs=[SMEM] + [VMEM] * 2,
        out_specs=(VMEM,) * 2,
        compiler_params=big,
        cost_estimate=pl.CostEstimate(flops=0, bytes_accessed=1 << 19, transcendentals=0),
        name="split",
    )(me, keys, values)
    b0, b1 = row_step(mine, 1), row_step(give, 1, 1)
    a1 = partner(give, 1)
    to_a, queries = lax.optimization_barrier((jnp.stack([mine, a1]), queries))
    qg = pl.pallas_call(
        pack_kernel,
        out_shape=jax.ShapeDtypeStruct((NQ, BLK, 2 * HD), bf16),
        in_specs=[VMEM] * 2,
        out_specs=VMEM,
        compiler_params=big,
        cost_estimate=pl.CostEstimate(flops=0, bytes_accessed=1 << 20, transcendentals=0),
        name="pack",
    )(queries, grad_out)
    qg = exchange(qg, XC_GROUPS)
    a23, group_lengths = lax.optimization_barrier((partner(to_a, 2), group_lengths))
    kv = [mine, a1, a23, b0, b1, partner(b0, 2), partner(b1, 2)]

    low, high = key_ranges(group_lengths, row, y_lo)
    lohi = jnp.stack([low, high], axis=1)
    base_a = (row * ROW + x * COL) * BLK
    base_b = base_a - ROW * BLK
    base = jnp.where(jnp.arange(NQ, dtype=jnp.int32) < x * NC, base_b, base_a)
    tile_first = jnp.clip((low[:, 0] - base) // BLK, 0, COL)
    tile_last = jnp.clip((high[:, -1] - base + BLK - 1) // BLK, 0, COL)
    info = jnp.concatenate([jnp.stack([x, base_a, base_b, y_lo, core, x, x, x]), tile_first, tile_last]).astype(jnp.int32)

    stats = stats_call(info, qg, kv, lohi)
    stats = exchange(stats, X_GROUPS)

    dq, own_a, own_b, away_a, away_b = grads_call(info, qg, kv, lohi, stats)

    got_b = partner(away_b, 2)
    dq = exchange(dq, XC_GROUPS)
    mine_b, other_b = [(own_b[i] + got_b[i].astype(jnp.float32)).astype(bf16) for i in range(NC)]
    mine_b, other_b, away_a = lax.optimization_barrier((mine_b, other_b, away_a))
    next_mine = row_step(mine_b, -1)
    other_b, dq = lax.optimization_barrier((other_b, dq))
    next_other = row_step(other_b, -1, 1)
    got_a = partner(away_a, 2)
    mate_a = partner((own_a[1] + got_a[1].astype(jnp.float32)).astype(bf16), 1)
    return pl.pallas_call(
        finish_kernel,
        out_shape=(jax.ShapeDtypeStruct((BLK, HEADS * HD), bf16),) * 3,
        in_specs=[SMEM] + [VMEM] * 6,
        out_specs=(VMEM,) * 3,
        compiler_params=PARAMS,
        cost_estimate=pl.CostEstimate(flops=0, bytes_accessed=2 << 20, transcendentals=0),
        name="finish",
    )(me, own_a, got_a, mate_a, next_mine, next_other, dq)


def solution(mesh):
    placed = P(("outer", "inner"), None)
    return jax.shard_map(
        per_device,
        mesh=mesh,
        in_specs=(placed, placed, placed, placed, P()),
        out_specs=(placed, placed, placed),
        check_vma=False,
    )
```

```python
import functools
import math

import jax
import jax.numpy as jnp
from jax import lax
from jax.experimental import pallas as pl
from jax.experimental.pallas import tpu as pltpu
from jax.sharding import PartitionSpec as P

HEADS = 2
HD = 128
CTX = 2
BLK = 256
NX, NY, NC = 4, 2, 2
ROW = NX * NY * NC
COL = NY * NC
NQ = NX * NC
NEG = -1e30
UNROLL = 4
LOG2E = math.log2(math.e)

XC_GROUPS = [[x * 4 + y * 2 + c for x in range(NX) for c in range(NC)] for y in range(NY)]
X_GROUPS = [[x * 4 + k for x in range(NX)] for k in range(COL)]


def exchange(value, groups):
    return lax.all_to_all(value, "inner", 0, 0, axis_index_groups=groups, tiled=True)


def row_step(value, steps, flip=0):
    count = lax.axis_size("outer")
    first, last = max(0, -steps), min(count, count - steps)
    route = [(r * ROW + i, (r + steps) * ROW + (i ^ flip)) for r in range(first, last) for i in range(ROW)]
    return lax.ppermute(value, ("outer", "inner"), route)


def partner(value, flip):
    return lax.ppermute(value, "inner", [(i ^ flip, i) for i in range(ROW)])


def key_ranges(group_lengths, row, y_lo):
    ends = jnp.cumsum(group_lengths).astype(jnp.int32)
    x = jnp.arange(NX, dtype=jnp.int32)[:, None, None]
    c = jnp.arange(NC, dtype=jnp.int32)[None, :, None]
    i = jnp.arange(BLK, dtype=jnp.int32)[None, None, :]
    first = (row * ROW + x * COL + y_lo * NC + c) * BLK
    pos = (first + i).reshape(NQ, BLK)
    last = (first + BLK + 0 * i).reshape(NQ, BLK)
    e = ends[:, None, None]
    low = jnp.max(jnp.where(e[CTX:] <= pos[None], e[:-CTX], 0), axis=0)
    high = jnp.min(jnp.where(e > pos[None], e, jnp.int32(1 << 30)), axis=0)
    return low, jnp.minimum(high, last)


def list_tiles(info_ref, tiles_ref):
    x = info_ref[0]
    count = jnp.int32(0)
    for n in range(NQ):
        before = n // NC < x
        row = jnp.where(before, COL * BLK, 0)
        pos = jnp.where(before, info_ref[2], info_ref[1])

        def put(t, i, n=n, row=row, pos=pos):
            tiles_ref[0, i] = n
            tiles_ref[1, i] = row + t * BLK
            tiles_ref[2, i] = pos + t * BLK
            return i + 1

        count = lax.fori_loop(info_ref[8 + n], info_ref[16 + n], put, count)
    for i in range(UNROLL - 1):
        tiles_ref[0, count + i] = 0
        tiles_ref[1, count + i] = 0
        tiles_ref[2, count + i] = -(1 << 30)
    return (count + UNROLL - 1) // UNROLL


def tile_terms(tiles_ref, i, kv_ref, qg_ref, lohi_ref):
    n, row, pos = tiles_ref[0, i], tiles_ref[1, i], tiles_ref[2, i]
    rows = pl.ds(pl.multiple_of(row, BLK), BLK)
    k = kv_ref[rows, :HD]
    v = kv_ref[rows, HD:]
    q = qg_ref[n, :, :HD]
    g = qg_ref[n, :, HD:]
    dims = (((1,), (1,)), ((), ()))
    s = lax.dot_general(k, q, dims, preferred_element_type=jnp.float32) * (LOG2E / math.sqrt(HD))
    dp = lax.dot_general(v, g, dims, preferred_element_type=jnp.float32)
    key = lax.broadcasted_iota(jnp.int32, (BLK, BLK), 0)
    low = lohi_ref[n, 0:1]
    width = (lohi_ref[n, 1:2] - low).astype(jnp.uint32)
    allowed = (key - (low - pos)).astype(jnp.uint32) < width
    return n, rows, q, g, jnp.where(allowed, s, NEG), dp


def split_kernel(info_ref, k_ref, v_ref, mine_ref, give_ref):
    core = info_ref[0]
    for c in range(NC):

        @pl.when(core == c)
        def _():
            for i, ref in enumerate((k_ref, v_ref)):
                cols = slice(i * HD, (i + 1) * HD)
                mine_ref[:, cols] = ref[:, c * HD : (c + 1) * HD]
                give_ref[:, cols] = ref[:, (1 - c) * HD : (2 - c) * HD]


def pack_kernel(q_ref, g_ref, qg_ref):
    for n in range(NQ):
        head = slice(n % HEADS * HD, (n % HEADS + 1) * HD)
        qg_ref[n, :, :HD] = q_ref[:, head]
        qg_ref[n, :, HD:] = g_ref[:, head]


def assemble(y_lo, core, refs, out_ref):
    for j, ref in enumerate(refs):
        y = y_lo ^ (j // NC % NY)
        row = j // COL * COL * BLK + (y * NC + (core ^ (j % NC))) * BLK
        out_ref[pl.ds(pl.multiple_of(row, BLK), BLK)] = ref[...]


def stats_kernel(
    info_ref, qg_ref, a0_ref, a1_ref, a23_ref, b0_ref, b1_ref, b2_ref, b3_ref, lohi_ref,
    out_ref, tiles_ref, kv_ref, m_ref, l_ref, u_ref,
):
    y_lo, core = info_ref[3], info_ref[4]
    pairs = list_tiles(info_ref, tiles_ref)
    blocks = (a0_ref, a1_ref, a23_ref.at[0], a23_ref.at[1], b0_ref, b1_ref, b2_ref, b3_ref)
    assemble(y_lo, core, blocks, kv_ref)
    m_ref[...] = jnp.full_like(m_ref, NEG)
    l_ref[...] = jnp.zeros_like(l_ref)
    u_ref[...] = jnp.zeros_like(u_ref)

    def step(i, _):
        terms = [tile_terms(tiles_ref, UNROLL * i + j, kv_ref, qg_ref, lohi_ref) for j in range(UNROLL)]
        parts = []
        for n, _, _, _, s, dp in terms:
            m = jnp.max(s, axis=0, keepdims=True)
            e = jnp.exp2(s - m)
            parts.append((n, m, jnp.sum(e, axis=0, keepdims=True), jnp.sum(e * dp, axis=0, keepdims=True)))
        for n, m, l, u in parts:
            old = m_ref[n]
            new = jnp.maximum(old, m)
            keep, add = jnp.exp2(old - new), jnp.exp2(m - new)
            m_ref[n] = new
            l_ref[n] = l_ref[n] * keep + l * add
            u_ref[n] = u_ref[n] * keep + u * add
        return 0

    lax.fori_loop(0, pairs, step, 0)
    for n in range(NQ):
        m = m_ref[n]
        l = jnp.where(m > 0.5 * NEG, l_ref[n], 1.0)
        lse, delta = m + jnp.log2(l), u_ref[n] / l
        for i in range(NX):
            out_ref[i, n, 0:1] = lse
            out_ref[i, n, 1:2] = delta


def grads_kernel(
    info_ref, qg_ref, a0_ref, a1_ref, a23_ref, b0_ref, b1_ref, b2_ref, b3_ref, lohi_ref, stats_ref,
    dq_ref, own_a_ref, own_b_ref, away_a_ref, away_b_ref,
    tiles_ref, kv_ref, kt_ref, acc_ref, dqt_ref, sums_ref,
):
    y_lo, core = info_ref[3], info_ref[4]
    scale = 1.0 / math.sqrt(HD)
    pairs = list_tiles(info_ref, tiles_ref)
    blocks = (a0_ref, a1_ref, a23_ref.at[0], a23_ref.at[1], b0_ref, b1_ref, b2_ref, b3_ref)
    assemble(y_lo, core, blocks, kv_ref)
    kt_ref[...] = kv_ref[:, :HD].T
    acc_ref[...] = jnp.zeros_like(acc_ref)
    dqt_ref[...] = jnp.zeros_like(dqt_ref)
    for n in range(NQ):
        part = [stats_ref[i, n] for i in range(NX)]
        top = functools.reduce(jnp.maximum, [p[0:1] for p in part])
        weights = [jnp.exp2(p[0:1] - top) for p in part]
        total = sum(weights)
        sums_ref[n, 0:1] = top + jnp.log2(total)
        sums_ref[n, 1:2] = sum(w * p[1:2] for w, p in zip(weights, part)) / total

    def step(i, _):
        terms = [tile_terms(tiles_ref, UNROLL * i + j, kv_ref, qg_ref, lohi_ref) for j in range(UNROLL)]
        parts = []
        for n, rows, q, g, s, dp in terms:
            p = jnp.exp2(s - sums_ref[n, 0:1])
            pb = p.astype(jnp.bfloat16)
            ds = (p * (dp - sums_ref[n, 1:2])).astype(jnp.bfloat16)
            dims = (((1,), (0,)), ((), ()))
            dv = lax.dot_general(pb, g, dims, preferred_element_type=jnp.float32)
            dk = lax.dot_general(ds, q, dims, preferred_element_type=jnp.float32)
            dq = lax.dot_general(kt_ref[:, rows], ds, dims, preferred_element_type=jnp.float32)
            parts.append((n, rows, dk, dv, dq))
        for n, rows, dk, dv, dq in parts:
            acc_ref[rows, :HD] += dk
            acc_ref[rows, HD:] += dv
            dqt_ref[n] += dq
        return 0

    lax.fori_loop(0, pairs, step, 0)
    for n in range(NQ):
        dq_ref[n] = (dqt_ref[n] * scale).astype(jnp.bfloat16)
    for i in range(NC):
        for start, own_ref, away_ref in ((0, own_a_ref, away_a_ref), (COL * BLK, own_b_ref, away_b_ref)):
            for y, out_ref in ((y_lo, own_ref), (1 - y_lo, away_ref)):
                rows = pl.ds(pl.multiple_of(start + (y * NC + (core ^ i)) * BLK, BLK), BLK)
                out_ref[i, :, :HD] = (acc_ref[rows, :HD] * scale).astype(out_ref.dtype)
                out_ref[i, :, HD:] = acc_ref[rows, HD:].astype(out_ref.dtype)


def finish_kernel(
    info_ref, own_a_ref, got_a_ref, mate_a_ref, next_mine_ref, next_other_ref, dq_ref, grad_q_ref, grad_k_ref, grad_v_ref
):
    core = info_ref[0]
    f32 = jnp.float32
    mine = own_a_ref[0] + got_a_ref[0].astype(f32) + next_mine_ref[...].astype(f32)
    other = mate_a_ref[...].astype(f32) + next_other_ref[...].astype(f32)
    for c in range(NC):

        @pl.when(core == c)
        def _():
            for h, part in ((c, mine), (1 - c, other)):
                cols = slice(h * HD, (h + 1) * HD)
                grad_k_ref[:, cols] = part[:, :HD].astype(jnp.bfloat16)
                grad_v_ref[:, cols] = part[:, HD:].astype(jnp.bfloat16)

    for h in range(HEADS):
        dq = sum(dq_ref[i * HEADS + h].astype(f32) for i in range(NX))
        grad_q_ref[:, h * HD : (h + 1) * HD] = dq.T.astype(jnp.bfloat16)


SMEM = pl.BlockSpec(memory_space=pltpu.SMEM)
VMEM = pl.BlockSpec(memory_space=pltpu.VMEM)
PARAMS = pltpu.CompilerParams(vmem_limit_bytes=24 * 1024 * 1024)


def stats_call(info, qg, kv, lohi):
    return pl.pallas_call(
        stats_kernel,
        out_shape=jax.ShapeDtypeStruct((NX, NQ, 2, BLK), jnp.float32),
        in_specs=[SMEM] + [VMEM] * 9,
        out_specs=VMEM,
        scratch_shapes=[
            pltpu.SMEM((3, NQ * COL + UNROLL), jnp.int32),
            pltpu.VMEM((2 * COL * BLK, 2 * HD), jnp.bfloat16),
        ]
        + [pltpu.VMEM((NQ, 1, BLK), jnp.float32)] * 3,
        compiler_params=PARAMS,
        cost_estimate=pl.CostEstimate(flops=16 * 2 * 2 * BLK * BLK * HD, bytes_accessed=2 << 20, transcendentals=16 * BLK * BLK),
        name="stats",
    )(info, qg, *kv, lohi)


def grads_call(info, qg, kv, lohi, stats):
    part = (NC, BLK, 2 * HD)
    return pl.pallas_call(
        grads_kernel,
        out_shape=(
            jax.ShapeDtypeStruct((NQ, HD, BLK), jnp.bfloat16),
            jax.ShapeDtypeStruct(part, jnp.float32),
            jax.ShapeDtypeStruct(part, jnp.float32),
            jax.ShapeDtypeStruct(part, jnp.bfloat16),
            jax.ShapeDtypeStruct(part, jnp.bfloat16),
        ),
        in_specs=[SMEM] + [VMEM] * 10,
        out_specs=(VMEM,) * 5,
        scratch_shapes=[
            pltpu.SMEM((3, NQ * COL + UNROLL), jnp.int32),
            pltpu.VMEM((2 * COL * BLK, 2 * HD), jnp.bfloat16),
            pltpu.VMEM((HD, 2 * COL * BLK), jnp.bfloat16),
            pltpu.VMEM((2 * COL * BLK, 2 * HD), jnp.float32),
            pltpu.VMEM((NQ, HD, BLK), jnp.float32),
            pltpu.VMEM((NQ, 2, BLK), jnp.float32),
        ],
        compiler_params=PARAMS,
        cost_estimate=pl.CostEstimate(flops=16 * 5 * 2 * BLK * BLK * HD, bytes_accessed=4 << 20, transcendentals=16 * BLK * BLK),
        name="grads",
    )(info, qg, *kv, lohi, stats)


def per_device(queries, keys, values, grad_out, group_lengths):
    row = lax.axis_index("outer").astype(jnp.int32)
    inner = lax.axis_index("inner").astype(jnp.int32)
    x, y_lo, core = inner // COL, inner // NC % NY, inner % NC

    bf16 = jnp.bfloat16
    me = core[None]
    big = pltpu.CompilerParams(vmem_limit_bytes=60 * 1024 * 1024)
    mine, give = pl.pallas_call(
        split_kernel,
        out_shape=(jax.ShapeDtypeStruct((BLK, 2 * HD), bf16),) * 2,
        in_specs=[SMEM] + [VMEM] * 2,
        out_specs=(VMEM,) * 2,
        compiler_params=big,
        cost_estimate=pl.CostEstimate(flops=0, bytes_accessed=1 << 19, transcendentals=0),
        name="split",
    )(me, keys, values)
    qg = pl.pallas_call(
        pack_kernel,
        out_shape=jax.ShapeDtypeStruct((NQ, BLK, 2 * HD), bf16),
        in_specs=[VMEM] * 2,
        out_specs=VMEM,
        compiler_params=big,
        cost_estimate=pl.CostEstimate(flops=0, bytes_accessed=1 << 20, transcendentals=0),
        name="pack",
    )(queries, grad_out)

    b0, b1 = row_step(mine, 1), row_step(give, 1, 1)
    a1 = partner(give, 1)
    qg = exchange(qg, XC_GROUPS)
    a23, group_lengths = lax.optimization_barrier((partner(jnp.stack([mine, a1]), 2), group_lengths))
    kv = [mine, a1, a23, b0, b1, partner(b0, 2), partner(b1, 2)]

    low, high = key_ranges(group_lengths, row, y_lo)
    lohi = jnp.stack([low, high], axis=1)
    base_a = (row * ROW + x * COL) * BLK
    base_b = base_a - ROW * BLK
    base = jnp.where(jnp.arange(NQ, dtype=jnp.int32) < x * NC, base_b, base_a)
    tile_first = jnp.clip((low[:, 0] - base) // BLK, 0, COL)
    tile_last = jnp.clip((high[:, -1] - base + BLK - 1) // BLK, 0, COL)
    info = jnp.concatenate([jnp.stack([x, base_a, base_b, y_lo, core, x, x, x]), tile_first, tile_last]).astype(jnp.int32)

    stats = stats_call(info, qg, kv, lohi)
    stats = exchange(stats, X_GROUPS)

    dq, own_a, own_b, away_a, away_b = grads_call(info, qg, kv, lohi, stats)

    got_b = partner(away_b, 2)
    dq = exchange(dq, XC_GROUPS)
    mine_b, other_b = [(own_b[i] + got_b[i].astype(jnp.float32)).astype(bf16) for i in range(NC)]
    mine_b, other_b, away_a = lax.optimization_barrier((mine_b, other_b, away_a))
    next_mine = row_step(mine_b, -1)
    other_b, dq = lax.optimization_barrier((other_b, dq))
    next_other = row_step(other_b, -1, 1)
    got_a = partner(away_a, 2)
    mate_a = partner((own_a[1] + got_a[1].astype(jnp.float32)).astype(bf16), 1)
    return pl.pallas_call(
        finish_kernel,
        out_shape=(jax.ShapeDtypeStruct((BLK, HEADS * HD), bf16),) * 3,
        in_specs=[SMEM] + [VMEM] * 6,
        out_specs=(VMEM,) * 3,
        compiler_params=PARAMS,
        cost_estimate=pl.CostEstimate(flops=0, bytes_accessed=2 << 20, transcendentals=0),
        name="finish",
    )(me, own_a, got_a, mate_a, next_mine, next_other, dq)


def solution(mesh):
    placed = P(("outer", "inner"), None)
    return jax.shard_map(
        per_device,
        mesh=mesh,
        in_specs=(placed, placed, placed, placed, P()),
        out_specs=(placed, placed, placed),
        check_vma=False,
    )
```

```python
import functools
import math

import jax
import jax.numpy as jnp
from jax import lax
from jax.experimental import pallas as pl
from jax.experimental.pallas import tpu as pltpu
from jax.sharding import PartitionSpec as P

HEADS = 2
HD = 128
CTX = 2
BLK = 256
NX, NY, NC = 4, 2, 2
ROW = NX * NY * NC
COL = NY * NC
NQ = NX * NC
NEG = -1e30
UNROLL = 4
LOG2E = math.log2(math.e)

XC_GROUPS = [[x * 4 + y * 2 + c for x in range(NX) for c in range(NC)] for y in range(NY)]
X_GROUPS = [[x * 4 + k for x in range(NX)] for k in range(COL)]


def exchange(value, groups):
    return lax.all_to_all(value, "inner", 0, 0, axis_index_groups=groups, tiled=True)


def row_step(value, steps, flip=0):
    count = lax.axis_size("outer")
    first, last = max(0, -steps), min(count, count - steps)
    route = [(r * ROW + i, (r + steps) * ROW + (i ^ flip)) for r in range(first, last) for i in range(ROW)]
    return lax.ppermute(value, ("outer", "inner"), route)


def partner(value, flip):
    return lax.ppermute(value, "inner", [(i ^ flip, i) for i in range(ROW)])


def key_ranges(group_lengths, row, y_lo):
    ends = jnp.cumsum(group_lengths).astype(jnp.int32)
    x = jnp.arange(NX, dtype=jnp.int32)[:, None, None]
    c = jnp.arange(NC, dtype=jnp.int32)[None, :, None]
    i = jnp.arange(BLK, dtype=jnp.int32)[None, None, :]
    first = (row * ROW + x * COL + y_lo * NC + c) * BLK
    pos = (first + i).reshape(NQ, BLK)
    last = (first + BLK + 0 * i).reshape(NQ, BLK)
    e = ends[:, None, None]
    low = jnp.max(jnp.where(e[CTX:] <= pos[None], e[:-CTX], 0), axis=0)
    high = jnp.min(jnp.where(e > pos[None], e, jnp.int32(1 << 30)), axis=0)
    return low, jnp.minimum(high, last)


def list_tiles(info_ref, tiles_ref, wanted=(False, True), start=0):
    x = info_ref[0]
    count = jnp.int32(0)
    for n in range(NQ):
        before = n // NC < x
        row = jnp.where(before, start, 0)
        pos = jnp.where(before, info_ref[2], info_ref[1])

        def put(t, i, n=n, row=row, pos=pos):
            tiles_ref[0, i] = n
            tiles_ref[1, i] = row + t * BLK
            tiles_ref[2, i] = pos + t * BLK
            return i + 1

        first, last = info_ref[8 + n], info_ref[16 + n]
        if len(wanted) == 1:
            last = jnp.where(before == wanted[0], last, first)
        count = lax.fori_loop(first, last, put, count)
    for i in range(UNROLL - 1):
        tiles_ref[0, count + i] = 0
        tiles_ref[1, count + i] = 0
        tiles_ref[2, count + i] = -(1 << 30)
    return (count + UNROLL - 1) // UNROLL


def tile_terms(tiles_ref, i, kv_ref, qg_ref, lohi_ref):
    n, row, pos = tiles_ref[0, i], tiles_ref[1, i], tiles_ref[2, i]
    rows = pl.ds(pl.multiple_of(row, BLK), BLK)
    k = kv_ref[rows, :HD]
    v = kv_ref[rows, HD:]
    q = qg_ref[n, :, :HD]
    g = qg_ref[n, :, HD:]
    dims = (((1,), (1,)), ((), ()))
    s = lax.dot_general(k, q, dims, preferred_element_type=jnp.float32) * (LOG2E / math.sqrt(HD))
    dp = lax.dot_general(v, g, dims, preferred_element_type=jnp.float32)
    key = lax.broadcasted_iota(jnp.int32, (BLK, BLK), 0)
    low = lohi_ref[n, 0:1]
    width = (lohi_ref[n, 1:2] - low).astype(jnp.uint32)
    allowed = (key - (low - pos)).astype(jnp.uint32) < width
    return n, rows, q, g, jnp.where(allowed, s, NEG), dp


def split_kernel(info_ref, k_ref, v_ref, mine_ref, give_ref):
    core = info_ref[0]
    for c in range(NC):

        @pl.when(core == c)
        def _():
            for i, ref in enumerate((k_ref, v_ref)):
                cols = slice(i * HD, (i + 1) * HD)
                mine_ref[:, cols] = ref[:, c * HD : (c + 1) * HD]
                give_ref[:, cols] = ref[:, (1 - c) * HD : (2 - c) * HD]


def pack_kernel(q_ref, g_ref, qg_ref):
    for n in range(NQ):
        head = slice(n % HEADS * HD, (n % HEADS + 1) * HD)
        qg_ref[n, :, :HD] = q_ref[:, head]
        qg_ref[n, :, HD:] = g_ref[:, head]


def assemble(y_lo, core, refs, out_ref):
    for j, ref in enumerate(refs):
        y = y_lo ^ (j // NC % NY)
        row = j // COL * COL * BLK + (y * NC + (core ^ (j % NC))) * BLK
        out_ref[pl.ds(pl.multiple_of(row, BLK), BLK)] = ref[...]


def stats_kernel(
    info_ref, qg_ref, a0_ref, a1_ref, a23_ref, b0_ref, b1_ref, b2_ref, b3_ref, lohi_ref,
    out_ref, tiles_ref, kv_ref, m_ref, l_ref, u_ref,
):
    y_lo, core = info_ref[3], info_ref[4]
    pairs = list_tiles(info_ref, tiles_ref, start=COL * BLK)
    blocks = (a0_ref, a1_ref, a23_ref.at[0], a23_ref.at[1], b0_ref, b1_ref, b2_ref, b3_ref)
    assemble(y_lo, core, blocks, kv_ref)
    m_ref[...] = jnp.full_like(m_ref, NEG)
    l_ref[...] = jnp.zeros_like(l_ref)
    u_ref[...] = jnp.zeros_like(u_ref)

    def step(i, _):
        terms = [tile_terms(tiles_ref, UNROLL * i + j, kv_ref, qg_ref, lohi_ref) for j in range(UNROLL)]
        parts = []
        for n, _, _, _, s, dp in terms:
            m = jnp.max(s, axis=0, keepdims=True)
            e = jnp.exp2(s - m)
            parts.append((n, m, jnp.sum(e, axis=0, keepdims=True), jnp.sum(e * dp, axis=0, keepdims=True)))
        for n, m, l, u in parts:
            old = m_ref[n]
            new = jnp.maximum(old, m)
            keep, add = jnp.exp2(old - new), jnp.exp2(m - new)
            m_ref[n] = new
            l_ref[n] = l_ref[n] * keep + l * add
            u_ref[n] = u_ref[n] * keep + u * add
        return 0

    lax.fori_loop(0, pairs, step, 0)
    for n in range(NQ):
        m = m_ref[n]
        l = jnp.where(m > 0.5 * NEG, l_ref[n], 1.0)
        lse, delta = m + jnp.log2(l), u_ref[n] / l
        for i in range(NX):
            out_ref[i, n, 0:1] = lse
            out_ref[i, n, 1:2] = delta


def grads_kernel(
    before, info_ref, qg_ref, lohi_ref, stats_ref, *refs
):
    block_refs, refs = refs[: 4 if before else 3], refs[4 if before else 3 :]
    dq_in_ref, refs = (refs[0], refs[1:]) if before else (None, refs)
    dq_ref, own_ref, away_ref, tiles_ref, kv_ref, kt_ref, acc_ref, dqt_ref, sums_ref = refs
    y_lo, core = info_ref[3], info_ref[4]
    scale = 1.0 / math.sqrt(HD)
    pairs = list_tiles(info_ref, tiles_ref, (before,))
    if not before:
        block_refs = (block_refs[0], block_refs[1], block_refs[2].at[0], block_refs[2].at[1])
    assemble(y_lo, core, block_refs, kv_ref)
    kt_ref[...] = kv_ref[:, :HD].T
    acc_ref[...] = jnp.zeros_like(acc_ref)
    dqt_ref[...] = jnp.zeros_like(dqt_ref)
    for n in range(NQ):
        part = [stats_ref[i, n] for i in range(NX)]
        top = functools.reduce(jnp.maximum, [p[0:1] for p in part])
        weights = [jnp.exp2(p[0:1] - top) for p in part]
        total = sum(weights)
        sums_ref[n, 0:1] = top + jnp.log2(total)
        sums_ref[n, 1:2] = sum(w * p[1:2] for w, p in zip(weights, part)) / total

    def step(i, _):
        terms = [tile_terms(tiles_ref, UNROLL * i + j, kv_ref, qg_ref, lohi_ref) for j in range(UNROLL)]
        parts = []
        for n, rows, q, g, s, dp in terms:
            p = jnp.exp2(s - sums_ref[n, 0:1])
            pb = p.astype(jnp.bfloat16)
            ds = (p * (dp - sums_ref[n, 1:2])).astype(jnp.bfloat16)
            dims = (((1,), (0,)), ((), ()))
            dv = lax.dot_general(pb, g, dims, preferred_element_type=jnp.float32)
            dk = lax.dot_general(ds, q, dims, preferred_element_type=jnp.float32)
            dq = lax.dot_general(kt_ref[:, rows], ds, dims, preferred_element_type=jnp.float32)
            parts.append((n, rows, dk, dv, dq))
        for n, rows, dk, dv, dq in parts:
            acc_ref[rows, :HD] += dk
            acc_ref[rows, HD:] += dv
            dqt_ref[n] += dq
        return 0

    lax.fori_loop(0, pairs, step, 0)
    for n in range(NQ):
        dq = dqt_ref[n] * scale
        if before:
            dq += dq_in_ref[n].astype(jnp.float32)
        dq_ref[n] = dq.astype(jnp.bfloat16)
    for i in range(NC):
        for y, out_ref in ((y_lo, own_ref), (1 - y_lo, away_ref)):
            rows = pl.ds(pl.multiple_of((y * NC + (core ^ i)) * BLK, BLK), BLK)
            out_ref[i, :, :HD] = (acc_ref[rows, :HD] * scale).astype(out_ref.dtype)
            out_ref[i, :, HD:] = acc_ref[rows, HD:].astype(out_ref.dtype)


def finish_kernel(
    info_ref, own_a_ref, got_a_ref, mate_a_ref, next_mine_ref, next_other_ref, dq_ref, grad_q_ref, grad_k_ref, grad_v_ref
):
    core = info_ref[0]
    f32 = jnp.float32
    mine = own_a_ref[0] + got_a_ref[0].astype(f32) + next_mine_ref[...].astype(f32)
    other = mate_a_ref[...].astype(f32) + next_other_ref[...].astype(f32)
    for c in range(NC):

        @pl.when(core == c)
        def _():
            for h, part in ((c, mine), (1 - c, other)):
                cols = slice(h * HD, (h + 1) * HD)
                grad_k_ref[:, cols] = part[:, :HD].astype(jnp.bfloat16)
                grad_v_ref[:, cols] = part[:, HD:].astype(jnp.bfloat16)

    for h in range(HEADS):
        dq = sum(dq_ref[i * HEADS + h].astype(f32) for i in range(NX))
        grad_q_ref[:, h * HD : (h + 1) * HD] = dq.T.astype(jnp.bfloat16)


SMEM = pl.BlockSpec(memory_space=pltpu.SMEM)
VMEM = pl.BlockSpec(memory_space=pltpu.VMEM)
PARAMS = pltpu.CompilerParams(vmem_limit_bytes=24 * 1024 * 1024)


def stats_call(info, qg, kv, lohi):
    return pl.pallas_call(
        stats_kernel,
        out_shape=jax.ShapeDtypeStruct((NX, NQ, 2, BLK), jnp.float32),
        in_specs=[SMEM] + [VMEM] * 9,
        out_specs=VMEM,
        scratch_shapes=[
            pltpu.SMEM((3, NQ * COL + UNROLL), jnp.int32),
            pltpu.VMEM((2 * COL * BLK, 2 * HD), jnp.bfloat16),
        ]
        + [pltpu.VMEM((NQ, 1, BLK), jnp.float32)] * 3,
        compiler_params=PARAMS,
        cost_estimate=pl.CostEstimate(flops=16 * 2 * 2 * BLK * BLK * HD, bytes_accessed=2 << 20, transcendentals=16 * BLK * BLK),
        name="stats",
    )(info, qg, *kv, lohi)


def grads_call(before, info, qg, lohi, stats, *more):
    part = (NC, BLK, 2 * HD)
    return pl.pallas_call(
        functools.partial(grads_kernel, before),
        out_shape=(
            jax.ShapeDtypeStruct((NQ, HD, BLK), jnp.bfloat16),
            jax.ShapeDtypeStruct(part, jnp.float32),
            jax.ShapeDtypeStruct(part, jnp.bfloat16),
        ),
        in_specs=[SMEM] + [VMEM] * (3 + len(more)),
        out_specs=(VMEM,) * 3,
        scratch_shapes=[
            pltpu.SMEM((3, NQ * COL + UNROLL), jnp.int32),
            pltpu.VMEM((COL * BLK, 2 * HD), jnp.bfloat16),
            pltpu.VMEM((HD, COL * BLK), jnp.bfloat16),
            pltpu.VMEM((COL * BLK, 2 * HD), jnp.float32),
            pltpu.VMEM((NQ, HD, BLK), jnp.float32),
            pltpu.VMEM((NQ, 2, BLK), jnp.float32),
        ],
        compiler_params=PARAMS,
        cost_estimate=pl.CostEstimate(flops=8 * 5 * 2 * BLK * BLK * HD, bytes_accessed=4 << 20, transcendentals=8 * BLK * BLK),
        name="grads_before" if before else "grads_own",
    )(info, qg, lohi, stats, *more)


def per_device(queries, keys, values, grad_out, group_lengths):
    row = lax.axis_index("outer").astype(jnp.int32)
    inner = lax.axis_index("inner").astype(jnp.int32)
    x, y_lo, core = inner // COL, inner // NC % NY, inner % NC

    bf16 = jnp.bfloat16
    me = core[None]
    big = pltpu.CompilerParams(vmem_limit_bytes=60 * 1024 * 1024)
    mine, give = pl.pallas_call(
        split_kernel,
        out_shape=(jax.ShapeDtypeStruct((BLK, 2 * HD), bf16),) * 2,
        in_specs=[SMEM] + [VMEM] * 2,
        out_specs=(VMEM,) * 2,
        compiler_params=big,
        cost_estimate=pl.CostEstimate(flops=0, bytes_accessed=1 << 19, transcendentals=0),
        name="split",
    )(me, keys, values)
    qg = pl.pallas_call(
        pack_kernel,
        out_shape=jax.ShapeDtypeStruct((NQ, BLK, 2 * HD), bf16),
        in_specs=[VMEM] * 2,
        out_specs=VMEM,
        compiler_params=big,
        cost_estimate=pl.CostEstimate(flops=0, bytes_accessed=1 << 20, transcendentals=0),
        name="pack",
    )(queries, grad_out)

    b0, b1 = row_step(mine, 1), row_step(give, 1, 1)
    a1 = partner(give, 1)
    qg = exchange(qg, XC_GROUPS)
    a23, group_lengths = lax.optimization_barrier((partner(jnp.stack([mine, a1]), 2), group_lengths))
    kv = [mine, a1, a23, b0, b1, partner(b0, 2), partner(b1, 2)]

    low, high = key_ranges(group_lengths, row, y_lo)
    lohi = jnp.stack([low, high], axis=1)
    base_a = (row * ROW + x * COL) * BLK
    base_b = base_a - ROW * BLK
    base = jnp.where(jnp.arange(NQ, dtype=jnp.int32) < x * NC, base_b, base_a)
    tile_first = jnp.clip((low[:, 0] - base) // BLK, 0, COL)
    tile_last = jnp.clip((high[:, -1] - base + BLK - 1) // BLK, 0, COL)
    info = jnp.concatenate([jnp.stack([x, base_a, base_b, y_lo, core, x, x, x]), tile_first, tile_last]).astype(jnp.int32)

    stats = stats_call(info, qg, kv, lohi)
    stats = exchange(stats, X_GROUPS)

    dq, own_a, away_a = grads_call(False, info, qg, lohi, stats, *kv[:3])
    got_a = partner(away_a, 2)
    dq, own_b, away_b = grads_call(True, info, qg, lohi, stats, *kv[3:], dq)
    away_b, got_a = lax.optimization_barrier((away_b, got_a))

    got_b = partner(away_b, 2)
    dq = exchange(dq, XC_GROUPS)
    mine_b, other_b = [(own_b[i] + got_b[i].astype(jnp.float32)).astype(bf16) for i in range(NC)]
    next_mine, next_other = row_step(mine_b, -1), row_step(other_b, -1, 1)
    mate_a = partner((own_a[1] + got_a[1].astype(jnp.float32)).astype(bf16), 1)
    return pl.pallas_call(
        finish_kernel,
        out_shape=(jax.ShapeDtypeStruct((BLK, HEADS * HD), bf16),) * 3,
        in_specs=[SMEM] + [VMEM] * 6,
        out_specs=(VMEM,) * 3,
        compiler_params=PARAMS,
        cost_estimate=pl.CostEstimate(flops=0, bytes_accessed=2 << 20, transcendentals=0),
        name="finish",
    )(me, own_a, got_a, mate_a, next_mine, next_other, dq)


def solution(mesh):
    placed = P(("outer", "inner"), None)
    return jax.shard_map(
        per_device,
        mesh=mesh,
        in_specs=(placed, placed, placed, placed, P()),
        out_specs=(placed, placed, placed),
        check_vma=False,
    )
```

```python
import functools
import math

import jax
import jax.numpy as jnp
from jax import lax
from jax.experimental import pallas as pl
from jax.experimental.pallas import tpu as pltpu
from jax.sharding import PartitionSpec as P

HEADS = 2
HD = 128
CTX = 2
BLK = 256
NX, NY, NC = 4, 2, 2
ROW = NX * NY * NC
COL = NY * NC
NQ = NX * NC
NEG = -1e30
UNROLL = 4
LOG2E = math.log2(math.e)

XC_GROUPS = [[x * 4 + y * 2 + c for x in range(NX) for c in range(NC)] for y in range(NY)]
X_GROUPS = [[x * 4 + k for x in range(NX)] for k in range(COL)]


def exchange(value, groups):
    return lax.all_to_all(value, "inner", 0, 0, axis_index_groups=groups, tiled=True)


def row_step(value, steps, flip=0):
    count = lax.axis_size("outer")
    first, last = max(0, -steps), min(count, count - steps)
    route = [(r * ROW + i, (r + steps) * ROW + (i ^ flip)) for r in range(first, last) for i in range(ROW)]
    return lax.ppermute(value, ("outer", "inner"), route)


def partner(value, flip):
    return lax.ppermute(value, "inner", [(i ^ flip, i) for i in range(ROW)])


def key_ranges(group_lengths, row, y_lo):
    ends = jnp.cumsum(group_lengths).astype(jnp.int32)
    x = jnp.arange(NX, dtype=jnp.int32)[:, None, None]
    c = jnp.arange(NC, dtype=jnp.int32)[None, :, None]
    i = jnp.arange(BLK, dtype=jnp.int32)[None, None, :]
    first = (row * ROW + x * COL + y_lo * NC + c) * BLK
    pos = (first + i).reshape(NQ, BLK)
    last = (first + BLK + 0 * i).reshape(NQ, BLK)
    e = ends[:, None, None]
    low = jnp.max(jnp.where(e[CTX:] <= pos[None], e[:-CTX], 0), axis=0)
    high = jnp.min(jnp.where(e > pos[None], e, jnp.int32(1 << 30)), axis=0)
    return low, jnp.minimum(high, last)


def list_tiles(info_ref, tiles_ref):
    x = info_ref[0]
    count = jnp.int32(0)
    for n in range(NQ):
        before = n // NC < x
        row = jnp.where(before, COL * BLK, 0)
        pos = jnp.where(before, info_ref[2], info_ref[1])

        def put(t, i, n=n, row=row, pos=pos):
            tiles_ref[0, i] = n
            tiles_ref[1, i] = row + t * BLK
            tiles_ref[2, i] = pos + t * BLK
            return i + 1

        count = lax.fori_loop(info_ref[8 + n], info_ref[16 + n], put, count)
    for i in range(UNROLL - 1):
        tiles_ref[0, count + i] = 0
        tiles_ref[1, count + i] = 0
        tiles_ref[2, count + i] = -(1 << 30)
    return (count + UNROLL - 1) // UNROLL


def tile_terms(tiles_ref, i, kv_ref, qg_ref, lohi_ref):
    n, row, pos = tiles_ref[0, i], tiles_ref[1, i], tiles_ref[2, i]
    rows = pl.ds(pl.multiple_of(row, BLK), BLK)
    k = kv_ref[rows, :HD]
    v = kv_ref[rows, HD:]
    q = qg_ref[n, :, :HD]
    g = qg_ref[n, :, HD:]
    dims = (((1,), (1,)), ((), ()))
    s = lax.dot_general(k, q, dims, preferred_element_type=jnp.float32) * (LOG2E / math.sqrt(HD))
    dp = lax.dot_general(v, g, dims, preferred_element_type=jnp.float32)
    key = lax.broadcasted_iota(jnp.int32, (BLK, BLK), 0)
    low = lohi_ref[n, 0:1]
    width = (lohi_ref[n, 1:2] - low).astype(jnp.uint32)
    allowed = (key - (low - pos)).astype(jnp.uint32) < width
    return n, rows, q, g, jnp.where(allowed, s, NEG), dp


def split_kernel(k_ref, v_ref, mine_ref, give_ref):
    core = lax.rem(lax.axis_index("inner"), NC)
    for c in range(NC):

        @pl.when(core == c)
        def _():
            for i, ref in enumerate((k_ref, v_ref)):
                cols = slice(i * HD, (i + 1) * HD)
                mine_ref[:, cols] = ref[:, c * HD : (c + 1) * HD]
                give_ref[:, cols] = ref[:, (1 - c) * HD : (2 - c) * HD]


def pack_kernel(q_ref, g_ref, qg_ref):
    for n in range(NQ):
        head = slice(n % HEADS * HD, (n % HEADS + 1) * HD)
        qg_ref[n, :, :HD] = q_ref[:, head]
        qg_ref[n, :, HD:] = g_ref[:, head]


def assemble(y_lo, core, refs, out_ref):
    for j, ref in enumerate(refs):
        y = y_lo ^ (j // NC % NY)
        row = j // COL * COL * BLK + (y * NC + (core ^ (j % NC))) * BLK
        out_ref[pl.ds(pl.multiple_of(row, BLK), BLK)] = ref[...]


def stats_kernel(
    info_ref, qg_ref, a0_ref, a1_ref, a23_ref, b0_ref, b1_ref, b2_ref, b3_ref, lohi_ref,
    out_ref, tiles_ref, kv_ref, m_ref, l_ref, u_ref,
):
    y_lo, core = info_ref[3], info_ref[4]
    pairs = list_tiles(info_ref, tiles_ref)
    blocks = (a0_ref, a1_ref, a23_ref.at[0], a23_ref.at[1], b0_ref, b1_ref, b2_ref, b3_ref)
    assemble(y_lo, core, blocks, kv_ref)
    m_ref[...] = jnp.full_like(m_ref, NEG)
    l_ref[...] = jnp.zeros_like(l_ref)
    u_ref[...] = jnp.zeros_like(u_ref)

    def step(i, _):
        terms = [tile_terms(tiles_ref, UNROLL * i + j, kv_ref, qg_ref, lohi_ref) for j in range(UNROLL)]
        parts = []
        for n, _, _, _, s, dp in terms:
            m = jnp.max(s, axis=0, keepdims=True)
            e = jnp.exp2(s - m)
            parts.append((n, m, jnp.sum(e, axis=0, keepdims=True), jnp.sum(e * dp, axis=0, keepdims=True)))
        for n, m, l, u in parts:
            old = m_ref[n]
            new = jnp.maximum(old, m)
            keep, add = jnp.exp2(old - new), jnp.exp2(m - new)
            m_ref[n] = new
            l_ref[n] = l_ref[n] * keep + l * add
            u_ref[n] = u_ref[n] * keep + u * add
        return 0

    lax.fori_loop(0, pairs, step, 0)
    for n in range(NQ):
        m = m_ref[n]
        l = jnp.where(m > 0.5 * NEG, l_ref[n], 1.0)
        lse, delta = m + jnp.log2(l), u_ref[n] / l
        for i in range(NX):
            out_ref[i, n, 0:1] = lse
            out_ref[i, n, 1:2] = delta


def grads_kernel(
    info_ref, qg_ref, a0_ref, a1_ref, a23_ref, b0_ref, b1_ref, b2_ref, b3_ref, lohi_ref, stats_ref,
    dq_ref, own_a_ref, own_b_ref, away_a_ref, away_b_ref,
    tiles_ref, kv_ref, kt_ref, acc_ref, dqt_ref, sums_ref,
):
    y_lo, core = info_ref[3], info_ref[4]
    scale = 1.0 / math.sqrt(HD)
    pairs = list_tiles(info_ref, tiles_ref)
    blocks = (a0_ref, a1_ref, a23_ref.at[0], a23_ref.at[1], b0_ref, b1_ref, b2_ref, b3_ref)
    assemble(y_lo, core, blocks, kv_ref)
    kt_ref[...] = kv_ref[:, :HD].T
    acc_ref[...] = jnp.zeros_like(acc_ref)
    dqt_ref[...] = jnp.zeros_like(dqt_ref)
    for n in range(NQ):
        part = [stats_ref[i, n] for i in range(NX)]
        top = functools.reduce(jnp.maximum, [p[0:1] for p in part])
        weights = [jnp.exp2(p[0:1] - top) for p in part]
        total = sum(weights)
        sums_ref[n, 0:1] = top + jnp.log2(total)
        sums_ref[n, 1:2] = sum(w * p[1:2] for w, p in zip(weights, part)) / total

    def step(i, _):
        terms = [tile_terms(tiles_ref, UNROLL * i + j, kv_ref, qg_ref, lohi_ref) for j in range(UNROLL)]
        parts = []
        for n, rows, q, g, s, dp in terms:
            p = jnp.exp2(s - sums_ref[n, 0:1])
            pb = p.astype(jnp.bfloat16)
            ds = (p * (dp - sums_ref[n, 1:2])).astype(jnp.bfloat16)
            dims = (((1,), (0,)), ((), ()))
            dv = lax.dot_general(pb, g, dims, preferred_element_type=jnp.float32)
            dk = lax.dot_general(ds, q, dims, preferred_element_type=jnp.float32)
            dq = lax.dot_general(kt_ref[:, rows], ds, dims, preferred_element_type=jnp.float32)
            parts.append((n, rows, dk, dv, dq))
        for n, rows, dk, dv, dq in parts:
            acc_ref[rows, :HD] += dk
            acc_ref[rows, HD:] += dv
            dqt_ref[n] += dq
        return 0

    lax.fori_loop(0, pairs, step, 0)
    for n in range(NQ):
        dq_ref[n] = (dqt_ref[n] * scale).astype(jnp.bfloat16)
    for i in range(NC):
        for start, own_ref, away_ref in ((0, own_a_ref, away_a_ref), (COL * BLK, own_b_ref, away_b_ref)):
            for y, out_ref in ((y_lo, own_ref), (1 - y_lo, away_ref)):
                rows = pl.ds(pl.multiple_of(start + (y * NC + (core ^ i)) * BLK, BLK), BLK)
                out_ref[i, :, :HD] = (acc_ref[rows, :HD] * scale).astype(out_ref.dtype)
                out_ref[i, :, HD:] = acc_ref[rows, HD:].astype(out_ref.dtype)


def finish_kernel(
    info_ref, own_a_ref, got_a_ref, mate_a_ref, next_mine_ref, next_other_ref, dq_ref, grad_q_ref, grad_k_ref, grad_v_ref
):
    core = info_ref[0]
    f32 = jnp.float32
    mine = own_a_ref[0].astype(f32) + got_a_ref[0].astype(f32) + next_mine_ref[...].astype(f32)
    other = mate_a_ref[...].astype(f32) + next_other_ref[...].astype(f32)
    for c in range(NC):

        @pl.when(core == c)
        def _():
            for h, part in ((c, mine), (1 - c, other)):
                cols = slice(h * HD, (h + 1) * HD)
                grad_k_ref[:, cols] = part[:, :HD].astype(jnp.bfloat16)
                grad_v_ref[:, cols] = part[:, HD:].astype(jnp.bfloat16)

    for h in range(HEADS):
        dq = sum(dq_ref[i * HEADS + h].astype(f32) for i in range(NX))
        grad_q_ref[:, h * HD : (h + 1) * HD] = dq.T.astype(jnp.bfloat16)


SMEM = pl.BlockSpec(memory_space=pltpu.SMEM)
VMEM = pl.BlockSpec(memory_space=pltpu.VMEM)
PARAMS = pltpu.CompilerParams(vmem_limit_bytes=24 * 1024 * 1024)


def stats_call(info, qg, kv, lohi):
    return pl.pallas_call(
        stats_kernel,
        out_shape=jax.ShapeDtypeStruct((NX, NQ, 2, BLK), jnp.float32),
        in_specs=[SMEM] + [VMEM] * 9,
        out_specs=VMEM,
        scratch_shapes=[
            pltpu.SMEM((3, NQ * COL + UNROLL), jnp.int32),
            pltpu.VMEM((2 * COL * BLK, 2 * HD), jnp.bfloat16),
        ]
        + [pltpu.VMEM((NQ, 1, BLK), jnp.float32)] * 3,
        compiler_params=PARAMS,
        cost_estimate=pl.CostEstimate(flops=16 * 2 * 2 * BLK * BLK * HD, bytes_accessed=2 << 20, transcendentals=16 * BLK * BLK),
        name="stats",
    )(info, qg, *kv, lohi)


def grads_call(info, qg, kv, lohi, stats):
    part = (NC, BLK, 2 * HD)
    return pl.pallas_call(
        grads_kernel,
        out_shape=(
            jax.ShapeDtypeStruct((NQ, HD, BLK), jnp.bfloat16),
            jax.ShapeDtypeStruct(part, jnp.bfloat16),
            jax.ShapeDtypeStruct(part, jnp.bfloat16),
            jax.ShapeDtypeStruct(part, jnp.bfloat16),
            jax.ShapeDtypeStruct(part, jnp.bfloat16),
        ),
        in_specs=[SMEM] + [VMEM] * 10,
        out_specs=(VMEM,) * 5,
        scratch_shapes=[
            pltpu.SMEM((3, NQ * COL + UNROLL), jnp.int32),
            pltpu.VMEM((2 * COL * BLK, 2 * HD), jnp.bfloat16),
            pltpu.VMEM((HD, 2 * COL * BLK), jnp.bfloat16),
            pltpu.VMEM((2 * COL * BLK, 2 * HD), jnp.float32),
            pltpu.VMEM((NQ, HD, BLK), jnp.float32),
            pltpu.VMEM((NQ, 2, BLK), jnp.float32),
        ],
        compiler_params=PARAMS,
        cost_estimate=pl.CostEstimate(flops=16 * 5 * 2 * BLK * BLK * HD, bytes_accessed=4 << 20, transcendentals=16 * BLK * BLK),
        name="grads",
    )(info, qg, *kv, lohi, stats)


def per_device(queries, keys, values, grad_out, group_lengths):
    row = lax.axis_index("outer").astype(jnp.int32)
    inner = lax.axis_index("inner").astype(jnp.int32)
    x, y_lo, core = inner // COL, inner // NC % NY, inner % NC

    bf16 = jnp.bfloat16
    me = core[None]
    big = pltpu.CompilerParams(vmem_limit_bytes=60 * 1024 * 1024)
    mine, give = pl.pallas_call(
        split_kernel,
        out_shape=(jax.ShapeDtypeStruct((BLK, 2 * HD), bf16),) * 2,
        in_specs=[VMEM] * 2,
        out_specs=(VMEM,) * 2,
        compiler_params=big,
        cost_estimate=pl.CostEstimate(flops=0, bytes_accessed=1 << 19, transcendentals=0),
        name="split",
    )(keys, values)
    qg = pl.pallas_call(
        pack_kernel,
        out_shape=jax.ShapeDtypeStruct((NQ, BLK, 2 * HD), bf16),
        in_specs=[VMEM] * 2,
        out_specs=VMEM,
        compiler_params=big,
        cost_estimate=pl.CostEstimate(flops=0, bytes_accessed=1 << 20, transcendentals=0),
        name="pack",
    )(queries, grad_out)

    b0, b1 = row_step(mine, 1), row_step(give, 1, 1)
    a1 = partner(give, 1)
    qg = exchange(qg, XC_GROUPS)
    a23 = partner(jnp.stack([mine, a1]), 2)
    b3, group_lengths = lax.optimization_barrier((partner(b1, 2), group_lengths))
    kv = [mine, a1, a23, b0, b1, partner(b0, 2), b3]

    low, high = key_ranges(group_lengths, row, y_lo)
    lohi = jnp.stack([low, high], axis=1)
    base_a = (row * ROW + x * COL) * BLK
    base_b = base_a - ROW * BLK
    base = jnp.where(jnp.arange(NQ, dtype=jnp.int32) < x * NC, base_b, base_a)
    tile_first = jnp.clip((low[:, 0] - base) // BLK, 0, COL)
    tile_last = jnp.clip((high[:, -1] - base + BLK - 1) // BLK, 0, COL)
    info = jnp.concatenate([jnp.stack([x, base_a, base_b, y_lo, core, x, x, x]), tile_first, tile_last]).astype(jnp.int32)

    stats = stats_call(info, qg, kv, lohi)
    stats = exchange(stats, X_GROUPS)

    dq, own_a, own_b, away_a, away_b = grads_call(info, qg, kv, lohi, stats)

    got_b = partner(away_b, 2)
    dq = exchange(dq, XC_GROUPS)
    mine_b, other_b = [(own_b[i].astype(jnp.float32) + got_b[i].astype(jnp.float32)).astype(bf16) for i in range(NC)]
    mine_b, other_b, away_a = lax.optimization_barrier((mine_b, other_b, away_a))
    next_mine = row_step(mine_b, -1)
    other_b, dq = lax.optimization_barrier((other_b, dq))
    next_other = row_step(other_b, -1, 1)
    got_a = partner(away_a, 2)
    mate_a = partner((own_a[1].astype(jnp.float32) + got_a[1].astype(jnp.float32)).astype(bf16), 1)
    return pl.pallas_call(
        finish_kernel,
        out_shape=(jax.ShapeDtypeStruct((BLK, HEADS * HD), bf16),) * 3,
        in_specs=[SMEM] + [VMEM] * 6,
        out_specs=(VMEM,) * 3,
        compiler_params=PARAMS,
        cost_estimate=pl.CostEstimate(flops=0, bytes_accessed=2 << 20, transcendentals=0),
        name="finish",
    )(me, own_a, got_a, mate_a, next_mine, next_other, dq)


def solution(mesh):
    placed = P(("outer", "inner"), None)
    return jax.shard_map(
        per_device,
        mesh=mesh,
        in_specs=(placed, placed, placed, placed, P()),
        out_specs=(placed, placed, placed),
        check_vma=False,
    )
```

```python
import functools
import math

import jax
import jax.numpy as jnp
from jax import lax
from jax.experimental import pallas as pl
from jax.experimental.pallas import tpu as pltpu
from jax.sharding import PartitionSpec as P

HEADS = 2
HD = 128
CTX = 2
BLK = 256
NX, NY, NC = 4, 2, 2
ROW = NX * NY * NC
COL = NY * NC
NQ = NX * NC
NEG = -1e30
UNROLL = 4
LOG2E = math.log2(math.e)

XC_GROUPS = [[x * 4 + y * 2 + c for x in range(NX) for c in range(NC)] for y in range(NY)]
X_GROUPS = [[x * 4 + k for x in range(NX)] for k in range(COL)]


def exchange(value, groups):
    return lax.all_to_all(value, "inner", 0, 0, axis_index_groups=groups, tiled=True)


def row_step(value, steps, flip=0):
    count = lax.axis_size("outer")
    first, last = max(0, -steps), min(count, count - steps)
    route = [(r * ROW + i, (r + steps) * ROW + (i ^ flip)) for r in range(first, last) for i in range(ROW)]
    return lax.ppermute(value, ("outer", "inner"), route)


def partner(value, flip):
    return lax.ppermute(value, "inner", [(i ^ flip, i) for i in range(ROW)])


def key_ranges(group_lengths, row, y_lo):
    ends = jnp.cumsum(group_lengths).astype(jnp.int32)
    x = jnp.arange(NX, dtype=jnp.int32)[:, None, None]
    c = jnp.arange(NC, dtype=jnp.int32)[None, :, None]
    i = jnp.arange(BLK, dtype=jnp.int32)[None, None, :]
    first = (row * ROW + x * COL + y_lo * NC + c) * BLK
    pos = (first + i).reshape(NQ, BLK)
    last = (first + BLK + 0 * i).reshape(NQ, BLK)
    e = ends[:, None, None]
    low = jnp.max(jnp.where(e[CTX:] <= pos[None], e[:-CTX], 0), axis=0)
    high = jnp.min(jnp.where(e > pos[None], e, jnp.int32(1 << 30)), axis=0)
    return low, jnp.minimum(high, last)


def list_tiles(info_ref, tiles_ref):
    x = info_ref[0]
    count = jnp.int32(0)
    for n in range(NQ):
        before = n // NC < x
        row = jnp.where(before, COL * BLK, 0)
        pos = jnp.where(before, info_ref[2], info_ref[1])

        def put(t, i, n=n, row=row, pos=pos):
            tiles_ref[0, i] = n
            tiles_ref[1, i] = row + t * BLK
            tiles_ref[2, i] = pos + t * BLK
            return i + 1

        count = lax.fori_loop(info_ref[8 + n], info_ref[16 + n], put, count)
    for i in range(UNROLL - 1):
        tiles_ref[0, count + i] = 0
        tiles_ref[1, count + i] = 0
        tiles_ref[2, count + i] = -(1 << 30)
    return (count + UNROLL - 1) // UNROLL


def tile_terms(tiles_ref, i, kv_ref, qg_ref, lohi_ref):
    n, row, pos = tiles_ref[0, i], tiles_ref[1, i], tiles_ref[2, i]
    rows = pl.ds(pl.multiple_of(row, BLK), BLK)
    k = kv_ref[rows, :HD]
    v = kv_ref[rows, HD:]
    q = qg_ref[n, :, :HD]
    g = qg_ref[n, :, HD:]
    dims = (((1,), (1,)), ((), ()))
    s = lax.dot_general(k, q, dims, preferred_element_type=jnp.float32) * (LOG2E / math.sqrt(HD))
    dp = lax.dot_general(v, g, dims, preferred_element_type=jnp.float32)
    key = lax.broadcasted_iota(jnp.int32, (BLK, BLK), 0)
    low = lohi_ref[n, 0:1]
    width = (lohi_ref[n, 1:2] - low).astype(jnp.uint32)
    allowed = (key - (low - pos)).astype(jnp.uint32) < width
    return n, rows, q, g, jnp.where(allowed, s, NEG), dp


def split_kernel(info_ref, k_ref, v_ref, mine_ref, give_ref):
    core = info_ref[0]
    for c in range(NC):

        @pl.when(core == c)
        def _():
            for i, ref in enumerate((k_ref, v_ref)):
                cols = slice(i * HD, (i + 1) * HD)
                mine_ref[:, cols] = ref[:, c * HD : (c + 1) * HD]
                give_ref[:, cols] = ref[:, (1 - c) * HD : (2 - c) * HD]


def pack_kernel(q_ref, g_ref, qg_ref):
    for n in range(NQ):
        head = slice(n % HEADS * HD, (n % HEADS + 1) * HD)
        qg_ref[n, :, :HD] = q_ref[:, head]
        qg_ref[n, :, HD:] = g_ref[:, head]


def assemble(y_lo, core, refs, out_ref):
    for j, ref in enumerate(refs):
        y = y_lo ^ (j // NC % NY)
        row = j // COL * COL * BLK + (y * NC + (core ^ (j % NC))) * BLK
        out_ref[pl.ds(pl.multiple_of(row, BLK), BLK)] = ref[...]


def stats_kernel(
    info_ref, qg_ref, a0_ref, a1_ref, a23_ref, b0_ref, b1_ref, b2_ref, b3_ref, lohi_ref,
    out_ref, tiles_ref, kv_ref, m_ref, l_ref, u_ref,
):
    y_lo, core = info_ref[3], info_ref[4]
    pairs = list_tiles(info_ref, tiles_ref)
    blocks = (a0_ref, a1_ref, a23_ref.at[0], a23_ref.at[1], b0_ref, b1_ref, b2_ref, b3_ref)
    assemble(y_lo, core, blocks, kv_ref)
    m_ref[...] = jnp.full_like(m_ref, NEG)
    l_ref[...] = jnp.zeros_like(l_ref)
    u_ref[...] = jnp.zeros_like(u_ref)

    def step(i, _):
        terms = [tile_terms(tiles_ref, UNROLL * i + j, kv_ref, qg_ref, lohi_ref) for j in range(UNROLL)]
        parts = []
        for n, _, _, _, s, dp in terms:
            m = jnp.max(s, axis=0, keepdims=True)
            e = jnp.exp2(s - m)
            parts.append((n, m, jnp.sum(e, axis=0, keepdims=True), jnp.sum(e * dp, axis=0, keepdims=True)))
        for n, m, l, u in parts:
            old = m_ref[n]
            new = jnp.maximum(old, m)
            keep, add = jnp.exp2(old - new), jnp.exp2(m - new)
            m_ref[n] = new
            l_ref[n] = l_ref[n] * keep + l * add
            u_ref[n] = u_ref[n] * keep + u * add
        return 0

    lax.fori_loop(0, pairs, step, 0)
    for n in range(NQ):
        m = m_ref[n]
        l = jnp.where(m > 0.5 * NEG, l_ref[n], 1.0)
        lse, delta = m + jnp.log2(l), u_ref[n] / l
        for i in range(NX):
            out_ref[i, n, 0:1] = lse
            out_ref[i, n, 1:2] = delta


def grads_kernel(
    info_ref, qg_ref, a0_ref, a1_ref, a23_ref, b0_ref, b1_ref, b2_ref, b3_ref, lohi_ref, stats_ref,
    dq_ref, own_a_ref, own_b_ref, away_a_ref, away_b_ref,
    tiles_ref, kv_ref, kt_ref, acc_ref, dqt_ref, sums_ref,
):
    y_lo, core = info_ref[3], info_ref[4]
    scale = 1.0 / math.sqrt(HD)
    pairs = list_tiles(info_ref, tiles_ref)
    blocks = (a0_ref, a1_ref, a23_ref.at[0], a23_ref.at[1], b0_ref, b1_ref, b2_ref, b3_ref)
    assemble(y_lo, core, blocks, kv_ref)
    kt_ref[...] = kv_ref[:, :HD].T
    acc_ref[...] = jnp.zeros_like(acc_ref)
    dqt_ref[...] = jnp.zeros_like(dqt_ref)
    for n in range(NQ):
        part = [stats_ref[i, n] for i in range(NX)]
        top = functools.reduce(jnp.maximum, [p[0:1] for p in part])
        weights = [jnp.exp2(p[0:1] - top) for p in part]
        total = sum(weights)
        sums_ref[n, 0:1] = top + jnp.log2(total)
        sums_ref[n, 1:2] = sum(w * p[1:2] for w, p in zip(weights, part)) / total

    def step(i, _):
        terms = [tile_terms(tiles_ref, UNROLL * i + j, kv_ref, qg_ref, lohi_ref) for j in range(UNROLL)]
        parts = []
        for n, rows, q, g, s, dp in terms:
            p = jnp.exp2(s - sums_ref[n, 0:1])
            pb = p.astype(jnp.bfloat16)
            ds = (p * (dp - sums_ref[n, 1:2])).astype(jnp.bfloat16)
            dims = (((1,), (0,)), ((), ()))
            dv = lax.dot_general(pb, g, dims, preferred_element_type=jnp.float32)
            dk = lax.dot_general(ds, q, dims, preferred_element_type=jnp.float32)
            dq = lax.dot_general(kt_ref[:, rows], ds, dims, preferred_element_type=jnp.float32)
            parts.append((n, rows, dk, dv, dq))
        for n, rows, dk, dv, dq in parts:
            acc_ref[rows, :HD] += dk
            acc_ref[rows, HD:] += dv
            dqt_ref[n] += dq
        return 0

    lax.fori_loop(0, pairs, step, 0)
    for n in range(NQ):
        dq_ref[n] = (dqt_ref[n] * scale).astype(jnp.bfloat16)
    for i in range(NC):
        for start, own_ref, away_ref in ((0, own_a_ref, away_a_ref), (COL * BLK, own_b_ref, away_b_ref)):
            for y, out_ref in ((y_lo, own_ref), (1 - y_lo, away_ref)):
                rows = pl.ds(pl.multiple_of(start + (y * NC + (core ^ i)) * BLK, BLK), BLK)
                out_ref[i, :, :HD] = (acc_ref[rows, :HD] * scale).astype(out_ref.dtype)
                out_ref[i, :, HD:] = acc_ref[rows, HD:].astype(out_ref.dtype)


def finish_q_kernel(dq_ref, grad_q_ref):
    for h in range(HEADS):
        dq = sum(dq_ref[i * HEADS + h].astype(jnp.float32) for i in range(NX))
        grad_q_ref[:, h * HD : (h + 1) * HD] = dq.T.astype(jnp.bfloat16)


def finish_kv_kernel(
    info_ref, own_a_ref, got_a_ref, mate_a_ref, next_mine_ref, next_other_ref, grad_k_ref, grad_v_ref
):
    core = info_ref[0]
    f32 = jnp.float32
    mine = own_a_ref[0] + got_a_ref[0].astype(f32) + next_mine_ref[...].astype(f32)
    other = mate_a_ref[...].astype(f32) + next_other_ref[...].astype(f32)
    for c in range(NC):

        @pl.when(core == c)
        def _():
            for h, part in ((c, mine), (1 - c, other)):
                cols = slice(h * HD, (h + 1) * HD)
                grad_k_ref[:, cols] = part[:, :HD].astype(jnp.bfloat16)
                grad_v_ref[:, cols] = part[:, HD:].astype(jnp.bfloat16)


SMEM = pl.BlockSpec(memory_space=pltpu.SMEM)
VMEM = pl.BlockSpec(memory_space=pltpu.VMEM)
PARAMS = pltpu.CompilerParams(vmem_limit_bytes=24 * 1024 * 1024)


def stats_call(info, qg, kv, lohi):
    return pl.pallas_call(
        stats_kernel,
        out_shape=jax.ShapeDtypeStruct((NX, NQ, 2, BLK), jnp.float32),
        in_specs=[SMEM] + [VMEM] * 9,
        out_specs=VMEM,
        scratch_shapes=[
            pltpu.SMEM((3, NQ * COL + UNROLL), jnp.int32),
            pltpu.VMEM((2 * COL * BLK, 2 * HD), jnp.bfloat16),
        ]
        + [pltpu.VMEM((NQ, 1, BLK), jnp.float32)] * 3,
        compiler_params=PARAMS,
        cost_estimate=pl.CostEstimate(flops=16 * 2 * 2 * BLK * BLK * HD, bytes_accessed=2 << 20, transcendentals=16 * BLK * BLK),
        name="stats",
    )(info, qg, *kv, lohi)


def grads_call(info, qg, kv, lohi, stats):
    part = (NC, BLK, 2 * HD)
    return pl.pallas_call(
        grads_kernel,
        out_shape=(
            jax.ShapeDtypeStruct((NQ, HD, BLK), jnp.bfloat16),
            jax.ShapeDtypeStruct(part, jnp.float32),
            jax.ShapeDtypeStruct(part, jnp.float32),
            jax.ShapeDtypeStruct(part, jnp.bfloat16),
            jax.ShapeDtypeStruct(part, jnp.bfloat16),
        ),
        in_specs=[SMEM] + [VMEM] * 10,
        out_specs=(VMEM,) * 5,
        scratch_shapes=[
            pltpu.SMEM((3, NQ * COL + UNROLL), jnp.int32),
            pltpu.VMEM((2 * COL * BLK, 2 * HD), jnp.bfloat16),
            pltpu.VMEM((HD, 2 * COL * BLK), jnp.bfloat16),
            pltpu.VMEM((2 * COL * BLK, 2 * HD), jnp.float32),
            pltpu.VMEM((NQ, HD, BLK), jnp.float32),
            pltpu.VMEM((NQ, 2, BLK), jnp.float32),
        ],
        compiler_params=PARAMS,
        cost_estimate=pl.CostEstimate(flops=16 * 5 * 2 * BLK * BLK * HD, bytes_accessed=4 << 20, transcendentals=16 * BLK * BLK),
        name="grads",
    )(info, qg, *kv, lohi, stats)


def per_device(queries, keys, values, grad_out, group_lengths):
    row = lax.axis_index("outer").astype(jnp.int32)
    inner = lax.axis_index("inner").astype(jnp.int32)
    x, y_lo, core = inner // COL, inner // NC % NY, inner % NC

    bf16 = jnp.bfloat16
    me = core[None]
    big = pltpu.CompilerParams(vmem_limit_bytes=60 * 1024 * 1024)
    mine, give = pl.pallas_call(
        split_kernel,
        out_shape=(jax.ShapeDtypeStruct((BLK, 2 * HD), bf16),) * 2,
        in_specs=[SMEM] + [VMEM] * 2,
        out_specs=(VMEM,) * 2,
        compiler_params=big,
        cost_estimate=pl.CostEstimate(flops=0, bytes_accessed=1 << 19, transcendentals=0),
        name="split",
    )(me, keys, values)
    qg = pl.pallas_call(
        pack_kernel,
        out_shape=jax.ShapeDtypeStruct((NQ, BLK, 2 * HD), bf16),
        in_specs=[VMEM] * 2,
        out_specs=VMEM,
        compiler_params=big,
        cost_estimate=pl.CostEstimate(flops=0, bytes_accessed=1 << 20, transcendentals=0),
        name="pack",
    )(queries, grad_out)

    b0, b1 = row_step(mine, 1), row_step(give, 1, 1)
    a1 = partner(give, 1)
    qg = exchange(qg, XC_GROUPS)
    a23 = partner(jnp.stack([mine, a1]), 2)
    b3, group_lengths = lax.optimization_barrier((partner(b1, 2), group_lengths))
    kv = [mine, a1, a23, b0, b1, partner(b0, 2), b3]

    low, high = key_ranges(group_lengths, row, y_lo)
    lohi = jnp.stack([low, high], axis=1)
    base_a = (row * ROW + x * COL) * BLK
    base_b = base_a - ROW * BLK
    base = jnp.where(jnp.arange(NQ, dtype=jnp.int32) < x * NC, base_b, base_a)
    tile_first = jnp.clip((low[:, 0] - base) // BLK, 0, COL)
    tile_last = jnp.clip((high[:, -1] - base + BLK - 1) // BLK, 0, COL)
    info = jnp.concatenate([jnp.stack([x, base_a, base_b, y_lo, core, x, x, x]), tile_first, tile_last]).astype(jnp.int32)

    stats = stats_call(info, qg, kv, lohi)
    stats = exchange(stats, X_GROUPS)

    dq, own_a, own_b, away_a, away_b = grads_call(info, qg, kv, lohi, stats)

    got_b = partner(away_b, 2)
    dq = exchange(dq, XC_GROUPS)
    mine_b, other_b = [(own_b[i] + got_b[i].astype(jnp.float32)).astype(bf16) for i in range(NC)]
    mine_b, other_b, away_a = lax.optimization_barrier((mine_b, other_b, away_a))
    next_mine = row_step(mine_b, -1)
    other_b, dq = lax.optimization_barrier((other_b, dq))
    next_other = row_step(other_b, -1, 1)
    got_a = partner(away_a, 2)
    mate_a = partner((own_a[1] + got_a[1].astype(jnp.float32)).astype(bf16), 1)
    whole = jax.ShapeDtypeStruct((BLK, HEADS * HD), bf16)
    grad_q = pl.pallas_call(
        finish_q_kernel,
        out_shape=whole,
        in_specs=[VMEM],
        out_specs=VMEM,
        compiler_params=PARAMS,
        cost_estimate=pl.CostEstimate(flops=0, bytes_accessed=1 << 20, transcendentals=0),
        name="finish_q",
    )(dq)
    grad_k, grad_v = pl.pallas_call(
        finish_kv_kernel,
        out_shape=(whole, whole),
        in_specs=[SMEM] + [VMEM] * 5,
        out_specs=(VMEM,) * 2,
        compiler_params=PARAMS,
        cost_estimate=pl.CostEstimate(flops=0, bytes_accessed=2 << 20, transcendentals=0),
        name="finish_kv",
    )(me, own_a, got_a, mate_a, next_mine, next_other)
    return grad_q, grad_k, grad_v


def solution(mesh):
    placed = P(("outer", "inner"), None)
    return jax.shard_map(
        per_device,
        mesh=mesh,
        in_specs=(placed, placed, placed, placed, P()),
        out_specs=(placed, placed, placed),
        check_vma=False,
    )
```
